128 devices in a mesh: rock: 8 (over y, core), plane: 16 (over z, x).
Axes of the slice: x: 4, y: 4, z: 4, core: 2. Of those that a mesh axis runs over, the one named last changes fastest.
Arguments:
- rock_state: float32 [36, 262144], P(None, ('rock', 'plane')), may hold values from -6 to 6
- jacobian: float32 [262144], P(('rock', 'plane')), may hold values from 0.5 to 2
- stiffness: float32 [36, 36], replicated, may hold values from -1 to 1
- trace_map: float32 [36, 36], replicated, may hold values from -1 to 1
- lift_map: float32 [36, 36], replicated, may hold values from -1 to 1
- neighbor_elem: int32 [4, 262144], P(None, ('rock', 'plane')), may hold values from 0 to 4095
- neighbor_face: int32 [4, 262144], P(None, ('rock', 'plane')), may hold values from 0 to 3
- send_elem: int32 [2, 131072], P(None, ('rock', 'plane')), may hold values from 0 to 2047
- opening_dir: float32 [36], replicated, may hold values from -1 to 1
- traction_dir: float32 [36], replicated, may hold values from -4 to 4
- face_elem: int32 [1048576], P(('rock', 'plane')), may hold values from 0 to 2047
- face_tile: int32 [1048576], P(('rock', 'plane')), may hold values from 0 to 15, as said below
- face_cell: int32 [1048576], P(('rock', 'plane')), may hold values from 0 to 16383
- face_count: int32 [128], P(('rock', 'plane')), may hold values from 2048 to 8192, as said below
- pressure: float32 [8, 32, 8192], P('rock', 'plane'), may hold values from -6 to 6
- base_aperture: float32 [8, 32, 8192], P('rock', 'plane'), may hold values from 0.4 to 1.2
- injection: float32 [8, 32, 8192], P('rock', 'plane'), may hold values from -6 to 6
Outputs:
- new_state: float32 [36, 262144], P(None, ('rock', 'plane'))
- new_pressure: float32 [8, 32, 8192], P('rock', 'plane')
- aperture: float32 [8, 32, 8192], P('rock', 'plane')
The draws below stay inside these ranges and needn't reach their ends.
Inputs may be any that keep to these rules, and one draw needn't show every extreme that they name: `face_tile`: each partition's 8192 slots name every tile exactly 512 times. `face_count`: some partition has all slots live.
All inputs are finite; a program needn't handle non-finite values.
Results may differ from the reference program's by a relative error of at most 0.00005.
Values sent between devices are 32-bit elements; how exact they have to be, the bound alone decides.
A program may use at most 64 MiB of HBM per device.

```python
import math
import jax
import jax.numpy as jnp
from jax import lax

Q = 36
E_DEV = 2048
HALO = 1024
ROWS_DEV = 2
FY = 8192
CAP = 512
ELEMS = 262144
HALO_ALL = 131072
NFRAC = 8
FX = 32
FACE_DEV = 8192
FACES = 1048576
N_ROCK = 8
N_PLANE = 16


def slot_orders(key):
    parts = N_ROCK * N_PLANE
    base_key = jax.random.fold_in(key, 7)
    return jax.vmap(lambda sub: jax.random.permutation(sub, FACE_DEV))(jax.random.split(base_key, parts))


def draw_face_tile(key, part):
    orders = slot_orders(key)
    return (orders // CAP).reshape(-1).astype(jnp.int32)


def draw_face_cell(key, part):
    orders = slot_orders(key)
    key = jax.random.fold_in(key, 11)
    parts = N_ROCK * N_PLANE
    inside = jax.random.randint(key, (parts, FACE_DEV), 0, ROWS_DEV * FY)
    inside = jnp.where(orders == 0, 0, inside)
    inside = jnp.where(orders == FACE_DEV - 1, ROWS_DEV * FY - 1, inside)
    return inside.reshape(-1).astype(jnp.int32)


def draw_face_count(key, part):
    key = jax.random.fold_in(key, 23)
    parts = N_ROCK * N_PLANE
    first_key, second_key = jax.random.split(key)
    counts = jax.random.randint(first_key, (parts,), FACE_DEV // 4, FACE_DEV + 1)
    order = jax.random.permutation(second_key, parts)
    counts = counts.at[order[0]].set(FACE_DEV).at[order[1]].set(FACE_DEV // 4)
    return counts.astype(jnp.int32)


def place_ends(result, rng, least, high):
    shape = result.shape
    index_at = [jax.random.randint(jax.random.fold_in(rng, axis), (), 0, shape[axis]) for axis in range(len(shape))]
    result = result.at[tuple(index_at)].set(least)
    longest = shape.index(max(shape))
    index_at[longest] = (index_at[longest] + 1) % shape[longest]
    return result.at[tuple(index_at)].set(high)


def block_scale(stream_key, shape, cuts, low, largest):
    def one(dim, blocks):
        heights = jax.random.uniform(jax.random.fold_in(jax.random.fold_in(stream_key, 6), dim), (blocks,), jnp.float32, low / len(cuts), largest / len(cuts))
        return jnp.repeat(jnp.exp(heights), shape[dim] // blocks).reshape((-1,) + (1,) * (len(shape) - dim - 1))

    factor_of = one(*cuts[0])
    for cut in cuts[1:]:
        factor_of = factor_of * one(*cut)
    return factor_of


def gaussian(stream_key, dims, spread, most, cuts=(), held_as=jnp.bfloat16):
    entries = spread * jax.random.normal(stream_key, dims, jnp.float32)
    if cuts:
        entries = entries * block_scale(stream_key, dims, cuts, -0.22, 0.18)
    return jnp.clip(entries, -most, most).astype(held_as)


def setup_inputs(seed: int = 0) -> dict:
    key_list = jax.random.split(jax.random.key(seed), 18)
    rock_state = gaussian(key_list[0], (Q, ELEMS), 1.0, 6.0, ((1, 128),), jnp.float32)
    jacobian = jnp.clip(jnp.exp(math.log(2.0) - 1.3862944 * jax.random.uniform(key_list[1], (ELEMS,), jnp.float32) ** block_scale(key_list[1], (ELEMS,), ((0, 128),), -0.2, 0.2)), 0.5, 2.0)
    stiffness = gaussian(key_list[2], (Q, Q), Q ** -0.5, 1.0, (), jnp.float32)
    trace_map = gaussian(key_list[3], (Q, Q), Q ** -0.5, 1.0, (), jnp.float32)
    lift_map = gaussian(key_list[4], (Q, Q), Q ** -0.5, 1.0, (), jnp.float32)
    neighbor_elem = place_ends(jax.random.randint(key_list[5], (4, ELEMS), 0, E_DEV + 2 * HALO), jax.random.fold_in(key_list[5], 1), 0, (E_DEV + 2 * HALO) - 1).astype(jnp.int32)
    neighbor_face = place_ends(jax.random.randint(key_list[6], (4, ELEMS), 0, 4), jax.random.fold_in(key_list[6], 1), 0, 3).astype(jnp.int32)
    send_elem = place_ends(jax.random.randint(key_list[7], (2, HALO_ALL), 0, E_DEV), jax.random.fold_in(key_list[7], 1), 0, E_DEV - 1).astype(jnp.int32)
    opening_dir = gaussian(key_list[8], (Q,), Q ** -0.5, 1.0, (), jnp.float32)
    traction_dir = gaussian(key_list[9], (Q,), 1.0, 4.0, (), jnp.float32)
    face_elem = place_ends(jax.random.randint(key_list[10], (FACES,), 0, E_DEV), jax.random.fold_in(key_list[10], 1), 0, E_DEV - 1).astype(jnp.int32)
    face_tile = draw_face_tile(jax.random.fold_in(key_list[17], 71), 0)
    face_cell = draw_face_cell(jax.random.fold_in(key_list[17], 71), 0)
    face_count = draw_face_count(jax.random.fold_in(key_list[17], 71), 0)
    pressure = gaussian(key_list[14], (NFRAC, FX, FY), 1.0, 6.0, ((0, 8), (1, 16)), jnp.float32)
    base_aperture = jnp.clip(jnp.exp(math.log(1.2) - 1.0986123 * jax.random.uniform(key_list[15], (NFRAC, FX, FY), jnp.float32) ** block_scale(key_list[15], (NFRAC, FX, FY), ((0, 8), (1, 16)), -0.2, 0.2)), 0.4, 1.2)
    injection = gaussian(key_list[16], (NFRAC, FX, FY), 1.0, 6.0, ((0, 8), (1, 16)), jnp.float32)
    return dict(rock_state=rock_state, jacobian=jacobian, stiffness=stiffness, trace_map=trace_map, lift_map=lift_map, neighbor_elem=neighbor_elem, neighbor_face=neighbor_face, send_elem=send_elem, opening_dir=opening_dir, traction_dir=traction_dir, face_elem=face_elem, face_tile=face_tile, face_cell=face_cell, face_count=face_count, pressure=pressure, base_aperture=base_aperture, injection=injection)


STEP = 0.25
RATE = 0.35


def neighbor_jumps(traces, lower_rim, upper_rim, near_elem, near_face):
    trace_pool = jnp.concatenate([traces, lower_rim, upper_rim], axis=1)
    width = traces.shape[0] // 4
    elements = traces.shape[1]
    pool_columns = trace_pool.shape[1]
    folded = trace_pool.reshape(4, width, pool_columns).transpose(1, 0, 2).reshape(width, 4 * pool_columns)
    flat_index = (near_face * pool_columns + near_elem).reshape(-1)
    chosen = folded[:, flat_index].reshape(width, 4, elements).transpose(1, 0, 2).reshape(4 * width, elements)
    return chosen - traces


def flux_sum(padded_p, padded_c):
    rows = padded_p.shape[0] - 2
    columns = padded_p.shape[1] - 2
    centre_p = padded_p[1:rows + 1, 1:columns + 1]
    centre_c = padded_c[1:rows + 1, 1:columns + 1]
    total = jnp.zeros((rows, columns), jnp.float32)
    for offset_row, offset_col in ((0, 1), (2, 1), (1, 0), (1, 2)):
        other_p = padded_p[offset_row:offset_row + rows, offset_col:offset_col + columns]
        other_c = padded_c[offset_row:offset_row + rows, offset_col:offset_col + columns]
        link = 2.0 * centre_c * other_c / (centre_c + other_c)
        total = total + link * (other_p - centre_p)
    return total


def elastic_step(state, jacobian, stiffness, trace_map, lift_map, neighbor_elem, neighbor_face, send_elem):
    parts = N_ROCK * N_PLANE
    traces = jnp.dot(trace_map, state, precision=lax.Precision.HIGHEST)
    per_part = traces.reshape(Q, parts, E_DEV).transpose(1, 0, 2)
    sends = send_elem.reshape(2, parts, HALO)
    picker = jax.vmap(lambda table, index: table[:, index])
    to_lower = picker(per_part, sends[0])
    to_upper = picker(per_part, sends[1])
    blank = jnp.zeros((1, Q, HALO), jnp.float32)
    from_lower = jnp.concatenate([blank, to_upper[:-1]], axis=0)
    from_upper = jnp.concatenate([to_lower[1:], blank], axis=0)
    states = state.reshape(Q, parts, E_DEV).transpose(1, 0, 2)
    scales = jacobian.reshape(parts, E_DEV)
    near_elem = neighbor_elem.reshape(4, parts, E_DEV).transpose(1, 0, 2)
    near_face = neighbor_face.reshape(4, parts, E_DEV).transpose(1, 0, 2)

    def one_part(items):
        own, own_traces, scale, elems, facets, lower_rim, upper_rim = items
        jumps = neighbor_jumps(own_traces, lower_rim, upper_rim, elems, facets)
        change = jnp.dot(stiffness, own, precision=lax.Precision.HIGHEST) + jnp.dot(lift_map, jumps, precision=lax.Precision.HIGHEST)
        return own + STEP * scale[None, :] * change

    updated = lax.map(one_part, (states, per_part, scales, near_elem, near_face, from_lower, from_upper))
    return updated.transpose(1, 0, 2).reshape(Q, ELEMS)


def reference(rock_state, jacobian, stiffness, trace_map, lift_map, neighbor_elem, neighbor_face, send_elem, opening_dir, traction_dir, face_elem, face_tile, face_cell, face_count, pressure, base_aperture, injection):
    parts = N_ROCK * N_PLANE
    state = elastic_step(rock_state, jacobian, stiffness, trace_map, lift_map, neighbor_elem, neighbor_face, send_elem)
    slots = face_elem.reshape(parts, FACE_DEV)
    cells = (face_tile * (ROWS_DEV * FY) + face_cell).reshape(parts, FACE_DEV)
    owners = jnp.arange(parts, dtype=jnp.int32)[:, None]
    live = jnp.arange(FACE_DEV, dtype=jnp.int32)[None, :] < face_count[:, None]
    global_elem = (owners * E_DEV + slots).reshape(-1)
    global_cell = ((owners // N_PLANE) * (FX * FY) + cells).reshape(-1)
    live = live.reshape(-1)
    scores = jnp.dot(opening_dir, state, precision=lax.Precision.HIGHEST)
    openings = jnp.where(live, 0.2 * jax.nn.softplus(scores[global_elem]), 0.0)
    aperture = base_aperture.reshape(-1).at[global_cell].add(openings).reshape(NFRAC, FX, FY)
    conduct = aperture * aperture * aperture / 12.0
    padded_p = jnp.pad(pressure, ((0, 0), (1, 1), (1, 1)))
    padded_c = jnp.pad(conduct, ((0, 0), (1, 1), (1, 1)))
    inflow = jax.vmap(flux_sum)(padded_p, padded_c)
    new_pressure = pressure + RATE * (inflow + injection)
    face_pressure = jnp.where(live, new_pressure.reshape(-1)[global_cell], 0.0)
    load = jnp.zeros((ELEMS,), jnp.float32).at[global_elem].add(face_pressure)
    loaded = state + STEP * (jacobian * load)[None, :] * traction_dir[:, None]
    new_state = elastic_step(loaded, jacobian, stiffness, trace_map, lift_map, neighbor_elem, neighbor_face, send_elem)
    return new_state, new_pressure, aperture
```

```python
import jax
import jax.numpy as jnp
from jax import lax
from jax.experimental import pallas as pl
from jax.experimental.pallas import tpu as pltpu
from jax.sharding import PartitionSpec as P

STEP = 0.25
RATE = 0.35
F32 = jnp.float32
BF16 = jnp.bfloat16
I32 = jnp.int32
MESH = pl.DeviceIdType.MESH
Q = 36
QP = 40
QB = 48
ELEMS = 2048
HALO = 1024
SLOTS = 8192
TILES = 16
PARTS = 128


def dot(a, b):
    return jnp.dot(a, b, preferred_element_type=F32)


def dot_nt(a, b):
    return lax.dot_general(a, b, (((1,), (1,)), ((), ())), preferred_element_type=F32)


def exact_dot(a, b):
    return jnp.dot(a, b, preferred_element_type=F32, precision=lax.Precision.HIGHEST)


def split(x):
    high = x.astype(BF16)
    return high, (x - high.astype(F32)).astype(BF16)


def iota(shape, dim):
    return lax.broadcasted_iota(I32, shape, dim)


def ones_where(mask):
    return jnp.where(mask, 1.0, 0.0).astype(F32)


def lanes(chunk, width=128):
    return pl.ds(pl.multiple_of(chunk * width, width), width)


def padded(x, rows):
    return jnp.concatenate([x, jnp.zeros((rows - x.shape[0],) + x.shape[1:], x.dtype)], axis=0)


def column(row):
    wide = jnp.broadcast_to(row, (QP, Q))
    eye = iota((QP, Q), 0) == iota((QP, Q), 1)
    return jnp.sum(jnp.where(eye, wide, 0.0), axis=1, keepdims=True)


def kernel(
    state_ref, jac_ref, stiff_ref, tmap_ref, lift_ref, nel_ref, nfa_ref, send_ref, odir_ref, tdir_ref,
    fel_ref, ftile_ref, fcell_ref, fcount_ref, press_ref, base_ref, inj_ref,
    new_state_ref, new_press_ref, aper_ref,
    s1, table, hot, send_hot, xh, xl, ww, tw, uu, out1, out2, rim1, rim2, wout, wrim,
    va, vb, elem_hot, elem_row, cells_out, cells_in, open_out, open_in, press_out, press_in,
    slot_tab, cell_hi, cell_lo, val, cond, edge_out, edge_in, edge_wide, change1, lane_row,
    halo_send, halo_recv, cell_send, cell_recv, open_send, open_recv, pr_send, pr_recv, edge_send, edge_recv,
):
    rock = lax.axis_index("rock")
    plane = lax.axis_index("plane")
    here = rock * TILES + plane
    nxt = lax.rem(here + 1, PARTS)
    prv = lax.rem(here + PARTS - 1, PARTS)
    next_part = (lax.div(nxt, TILES), lax.rem(nxt, TILES))
    prev_part = (lax.div(prv, TILES), lax.rem(prv, TILES))
    next_tile = (rock, lax.rem(plane + 1, TILES))
    prev_tile = (rock, lax.rem(plane + TILES - 1, TILES))

    def peer(o):
        return lax.rem(plane + o, TILES)

    barrier = pltpu.get_barrier_semaphore()
    for target in (next_part, prev_part):
        pl.semaphore_signal(barrier, inc=1, device_id=target, device_id_type=MESH)

    def greet(o, carry):
        pl.semaphore_signal(barrier, inc=1, device_id=(rock, peer(o)), device_id_type=MESH)
        return carry

    lax.fori_loop(1, TILES, greet, 0)

    def pair(outs, ins, index):
        return [
            pltpu.make_async_remote_copy(
                outs.at[0], ins.at[1], halo_send.at[index], halo_recv.at[index],
                device_id=prev_part, device_id_type=MESH),
            pltpu.make_async_remote_copy(
                outs.at[1], ins.at[0], halo_send.at[index + 1], halo_recv.at[index + 1],
                device_id=next_part, device_id_type=MESH),
        ]

    def edges(index):
        return [
            pltpu.make_async_remote_copy(
                edge_out.at[2 * index], edge_in.at[2 * index + 1], edge_send.at[2 * index],
                edge_recv.at[2 * index], device_id=prev_tile, device_id_type=MESH),
            pltpu.make_async_remote_copy(
                edge_out.at[2 * index + 1], edge_in.at[2 * index], edge_send.at[2 * index + 1],
                edge_recv.at[2 * index + 1], device_id=next_tile, device_id_type=MESH),
        ]

    def swap(outs, ins, sends, recvs, o):
        return pltpu.make_async_remote_copy(
            outs.at[peer(o)], ins.at[plane], sends.at[o - 1], recvs.at[o - 1],
            device_id=(rock, peer(o)), device_id_type=MESH)

    def start_all(*what):
        def one(o, carry):
            swap(*what, o).start()
            return carry
        lax.fori_loop(1, TILES, one, 0)
        outs, ins = what[:2]
        ins[plane] = outs[plane]

    def arrive_all(*what):
        def one(o, carry):
            swap(*what, o).wait_recv()
            return carry
        lax.fori_loop(1, TILES, one, 0)

    def sent_all(*what):
        def one(o, carry):
            swap(*what, o).wait_send()
            return carry
        lax.fori_loop(1, TILES, one, 0)

    tmap = tmap_ref[...]
    lift = lift_ref[...]
    th, tl = split(padded(tmap, QB))
    widen = ones_where(iota((Q, QB), 0) == iota((Q, QB), 1)).astype(BF16)
    tw[0:QB, :] = dot(th, widen).astype(BF16)
    tw[QB:2 * QB, :] = dot(tl, widen).astype(BF16)

    def put_state(x):
        high, rest = split(padded(x, QB))
        xh[0:QB, :] = high
        xl[0:QB, :] = rest

    def traces():
        first = dot(tw[...], xh[0:QB, :])
        return first[0:QP] + first[QB:QB + QP] + dot(tw[0:QB, :], xl[0:QB, :])[0:QP]

    def put_table(parts, start):
        rows = jnp.concatenate(
            [x[:, 256 * l:256 * l + 256] for x in parts for l in range(x.shape[1] // 256)], axis=0)
        high, rest = split(rows)
        table[start:start + rows.shape[0], 0:256] = high
        table[start:start + rows.shape[0], 256:512] = rest

    def pick(rows, which, count, height):
        got = rows[0:height]
        for l in range(1, count):
            got = jnp.where(which == l, rows[height * l:height * l + height], got)
        return got

    def fill_outgoing(out):
        for side in range(2):
            a = send_hot[:, HALO * side:HALO * side + HALO]
            rows = dot(table[0:320, :], jnp.concatenate([a, a], axis=0))
            out[side] = pick(rows, send_ref[side:side + 1, :] >> 8, 8, QP)

    def rims(rim):
        lower = jnp.where(here > 0, rim[0], 0.0)
        upper = jnp.where(here < PARTS - 1, rim[1], 0.0)
        return lower, upper

    face_of_row = lax.div(iota((QP, 1), 0), 9)

    def gather_faces(k):
        a = hot[:, ELEMS * k:ELEMS * k + ELEMS]
        rows = dot(table[...], jnp.concatenate([a, a], axis=0))
        got = pick(rows, nel_ref[k:k + 1, :] >> 8, 16, QP)
        got = jnp.where(face_of_row == nfa_ref[k:k + 1, :], got, 0.0)
        high, rest = split(padded(got, QB))
        xh[QB * (k + 1):QB * (k + 2), :] = high
        xl[QB * (k + 1):QB * (k + 2), :] = rest

    def change():
        first = dot(ww[...], xh[...])
        return first[0:QP] + first[QB:QB + QP] + dot(ww[0:QB, :], xl[...])[0:QP]

    s1[0:Q, :] = state_ref[...]
    s1[Q:QP, :] = jnp.zeros((QP - Q, ELEMS), F32)
    put_state(s1[...])
    tr = traces()
    put_table([tr], 0)

    def send_body(c, carry):
        for side in range(2):
            row = send_ref[side:side + 1, lanes(c)] & 255
            send_hot[:, lanes(8 * side + c)] = ones_where(iota((256, 128), 0) == row).astype(BF16)
        return carry

    lax.fori_loop(0, 8, send_body, 0, unroll=2)
    fill_outgoing(out1)
    pl.semaphore_wait(barrier, TILES + 1)
    for copy in pair(out1, rim1, 0):
        copy.start()
    edge_out[0] = press_ref[pl.ds(0, 64, stride=2), :]
    edge_out[1] = press_ref[pl.ds(1, 64, stride=2), :]
    for copy in edges(0):
        copy.start()

    tile = ftile_ref[...]
    upper = ones_where(iota((128, 128), 0) <= iota((128, 128), 1)).astype(BF16)
    count = jnp.concatenate([upper, jnp.ones((128, 128), BF16)], axis=0)
    before = ones_where(iota((64, 64), 1) < iota((64, 64), 0)).astype(BF16)
    named = [ones_where(tile == t).astype(BF16) for t in range(TILES)]
    earlier = dot(before, jnp.concatenate(named, axis=1)).astype(BF16)
    ranks = dot(
        jnp.concatenate(
            [jnp.concatenate([named[t], earlier[:, 128 * t:128 * t + 128]], axis=1) for t in range(TILES)],
            axis=0),
        count)
    place = jnp.zeros((64, 128), F32)
    for t in range(TILES):
        place = jnp.where(tile == t, ranks[64 * t:64 * t + 64] + (512.0 * t - 1.0), place)
    place = place.astype(I32)
    cell = fcell_ref[...]
    elem = fel_ref[...]
    slot = iota((64, 128), 0) * 128 + iota((64, 128), 1)
    live = jnp.where(slot < fcount_ref[0], 16, 0)
    slot_tab[0] = place >> 7
    slot_tab[1] = place & 127
    slot_tab[2] = ((cell >> 7) & 63) * 2 + (cell >> 13)
    slot_tab[3] = cell & 127
    slot_tab[4] = elem & 127
    slot_tab[5] = (elem >> 7) + live

    def order_body(c, carry):
        at = pl.ds(c, 1)
        mine = iota((64, 128), 0) == slot_tab[0, at, :]
        for v in range(4):
            va[64 * v:64 * v + 64, lanes(c)] = jnp.where(mine, slot_tab[2 + v, at, :], 0).astype(F32).astype(BF16)
        vb[0:128, lanes(c)] = ones_where(iota((128, 128), 0) == slot_tab[1, at, :]).astype(BF16)
        return carry

    lax.fori_loop(0, 64, order_body, 0, unroll=2)
    grouped = dot_nt(va[...], vb[0:128, :])
    code = grouped[0:64] * 128.0 + grouped[64:128]
    for t in range(TILES):
        cells_out[t] = code[4 * t:4 * t + 4]
    elem_row[0] = grouped[128:192]
    elem_row[1] = grouped[192:256]
    start_all(cells_out, cells_in, cell_send, cell_recv)

    def elem_body(c, carry):
        row = elem_row[0, pl.ds(c, 1), :]
        elem_hot[:, lanes(c)] = ones_where(iota((128, 128), 0).astype(F32) == row).astype(BF16)
        return carry

    lax.fori_loop(0, 64, elem_body, 0, unroll=2)

    for k in range(4):
        def hot_body(c, carry):
            row = nel_ref[k:k + 1, lanes(c)] & 255
            hot[:, lanes(16 * k + c)] = ones_where(iota((256, 128), 0) == row).astype(BF16)
            return carry

        lax.fori_loop(0, 16, hot_body, 0, unroll=2)

    row_i = iota((Q, 256), 0)
    col_i = iota((Q, 256), 1)
    own_block = ones_where(row_i == col_i).astype(BF16)
    blk = lax.div(col_i, QB)
    inner = lax.rem(col_i, QB)
    face_block = ones_where(
        (blk >= 1) & (blk <= 4) & (inner < Q) & (row_i == 9 * (blk - 1) + lax.rem(inner, 9))).astype(BF16)
    volume = stiff_ref[...] - exact_dot(lift, tmap)
    mh, ml = split(padded(volume, QB))
    lh, ll = split(padded(lift, QB))
    ww[0:QB, :] = (dot(mh, own_block) + dot(lh, face_block)).astype(BF16)
    ww[QB:2 * QB, :] = (dot(ml, own_block) + dot(ll, face_block)).astype(BF16)
    xh[5 * QB:256, :] = jnp.zeros((16, ELEMS), BF16)
    xl[5 * QB:256, :] = jnp.zeros((16, ELEMS), BF16)

    push = column(tdir_ref[...])
    tau = exact_dot(tmap, push[0:Q])
    same = ones_where(lax.rem(iota((Q, Q), 0), 9) == lax.rem(iota((Q, Q), 1), 9))
    of_facet = jnp.where(lax.div(iota((Q, 128), 0), 9) == lax.rem(iota((Q, 128), 1), 4), tau, 0.0)
    spread = jnp.where(
        lax.div(iota((Q, 128), 0), 9) == lax.div(iota((Q, 128), 1), 4), exact_dot(same, of_facet), 0.0)
    load_map = jnp.where(
        iota((Q, 128), 1) == 16, exact_dot(volume, push[0:Q]), exact_dot(lift, spread))
    uh, ul = split(padded(load_map, QB))
    uu[0:QB, :] = uh
    uu[QB:2 * QB, :] = ul

    for copy in pair(out1, rim1, 0):
        copy.wait_recv()
    put_table(list(rims(rim1)), 320)
    for k in range(4):
        gather_faces(k)
    scale = STEP * jac_ref[...]
    s1[...] = s1[...] + scale * change()

    score = jnp.sum(column(odir_ref[...]) * s1[...], axis=0, keepdims=True)
    opening = 0.2 * (jnp.maximum(score, 0.0) + jnp.log1p(jnp.exp(-jnp.abs(score))))
    oh, ol = split(jnp.concatenate([opening[:, 128 * i:128 * i + 128] for i in range(16)], axis=0))
    got = dot(jnp.concatenate([oh, ol], axis=0), elem_hot[...])
    val[0:16, :] = got[0:16] + got[16:32]
    sixteen = (iota((16, 128), 0) + 16).astype(F32)

    def open_body(t, carry):
        for r in range(4):
            mine = sixteen == elem_row[1, pl.ds(4 * t + r, 1), :]
            open_out[t, r:r + 1, :] = jnp.sum(
                jnp.where(mine, val[0:16, lanes(4 * t + r)], 0.0), axis=0, keepdims=True)
        return carry

    lax.fori_loop(0, TILES, open_body, 0, unroll=2)
    start_all(open_out, open_in, open_send, open_recv)

    put_state(s1[...])
    tr = traces()
    put_table([tr], 0)
    fill_outgoing(out2)
    for copy in pair(out2, rim2, 2):
        copy.start()

    arrive_all(cells_out, cells_in, cell_send, cell_recv)

    def cell_body(t, carry):
        for r in range(4):
            c = 4 * t + r
            at = cells_in[t, r:r + 1, :].astype(I32)
            cell_hi[:, lanes(c)] = ones_where(iota((128, 128), 0) == (at >> 7)).astype(BF16)
            cell_lo[:, lanes(c)] = ones_where(iota((128, 128), 0) == (at & 127)).astype(BF16)
        return carry

    lax.fori_loop(0, TILES, cell_body, 0)
    arrive_all(open_out, open_in, open_send, open_recv)

    def amount_body(t, carry):
        for r in range(4):
            c = 4 * t + r
            high, rest = split(jnp.broadcast_to(open_in[t, r:r + 1, :], (128, 128)))
            unit = cell_lo[:, lanes(c)]
            vb[0:128, lanes(c)] = unit * high
            vb[128:256, lanes(c)] = unit * rest
        return carry

    lax.fori_loop(0, TILES, amount_body, 0)
    field = dot_nt(cell_hi[...], vb[...])
    aper = base_ref[...] + (field[:, 0:128] + field[:, 128:256])
    aper_ref[...] = aper
    c = aper * aper * aper / 12.0
    cond[...] = c
    edge_out[2] = cond[pl.ds(0, 64, stride=2), :]
    edge_out[3] = cond[pl.ds(1, 64, stride=2), :]
    for copy in edges(1):
        copy.start()

    for copy in pair(out2, rim2, 2):
        copy.wait_recv()
    put_table(list(rims(rim2)), 320)
    gather_faces(0)

    p = press_ref[...]
    odd = (iota((128, 128), 0) & 1) == 1
    lane = iota((128, 128), 1)
    block = iota((128, 128), 0) >> 1
    for copy in edges(0) + edges(1):
        copy.wait_recv()
    for i in range(2):
        edge_wide[i, pl.ds(0, 64, stride=2), :] = edge_in[2 * i]
        edge_wide[i, pl.ds(1, 64, stride=2), :] = edge_in[2 * i + 1]

    def sides(x, wide):
        after = pltpu.roll(x, 127, 1)
        after = jnp.where(lane == 127, pltpu.roll(after, 126, 0), after)
        ahead = pltpu.roll(x, 1, 1)
        ahead = jnp.where(lane == 0, pltpu.roll(ahead, 2, 0), ahead)
        up = jnp.where(odd, pltpu.roll(x, 1, 0), wide)
        down = jnp.where(odd, wide, pltpu.roll(x, 127, 0))
        inside = (
            (lane < 127) | (block < 63),
            (lane > 0) | (block > 0),
            odd | (plane > 0),
            jnp.logical_not(odd) | (plane < TILES - 1),
        )
        return [jnp.where(m, v, 0.0) for m, v in zip(inside, (after, ahead, up, down))]

    inflow = jnp.zeros((128, 128), F32)
    for other_p, other_c in zip(sides(p, edge_wide[0]), sides(c, edge_wide[1])):
        inflow = inflow + 2.0 * c * other_c / (c + other_c) * (other_p - p)
    new_p = p + RATE * (inflow + inj_ref[...])
    new_press_ref[...] = new_p

    ph, prest = split(new_p)
    units = cell_lo[...]
    val[...] = dot(jnp.concatenate([ph, prest], axis=1), jnp.concatenate([units, units], axis=0))

    def press_body(t, carry):
        for r in range(4):
            mine = iota((128, 128), 0) == (cells_in[t, r:r + 1, :].astype(I32) >> 7)
            press_out[t, r:r + 1, :] = jnp.sum(
                jnp.where(mine, val[:, lanes(4 * t + r)], 0.0), axis=0, keepdims=True)
        return carry

    lax.fori_loop(0, TILES, press_body, 0)
    start_all(press_out, press_in, pr_send, pr_recv)
    gather_faces(1)
    gather_faces(2)
    arrive_all(press_out, press_in, pr_send, pr_recv)

    def load_body(t, carry):
        for r in range(4):
            c = 4 * t + r
            mine = sixteen == elem_row[1, pl.ds(c, 1), :]
            high, rest = split(jnp.where(mine, press_in[t, r:r + 1, :], 0.0))
            va[0:16, lanes(c)] = high
            va[16:32, lanes(c)] = rest
        return carry

    lax.fori_loop(0, TILES, load_body, 0, unroll=2)
    load = dot_nt(va[0:32, :], elem_hot[...])
    load = load[0:16] + load[16:32]
    for i in range(16):
        lane_row[:, 128 * i:128 * i + 128] = load[i:i + 1]
    w = scale * lane_row[...]
    own_w = jnp.concatenate([w[:, 256 * l:256 * l + 256] for l in range(8)], axis=0)
    wh, wl = split(own_w)
    got = dot(jnp.concatenate([wh, wl], axis=0), send_hot[...])
    got = got[0:8] + got[8:16]
    for side in range(2):
        mine = iota((8, HALO), 0) == (send_ref[side:side + 1, :] >> 8)
        wout[side] = jnp.sum(
            jnp.where(mine, got[:, HALO * side:HALO * side + HALO], 0.0), axis=0, keepdims=True)
    for copy in pair(wout, wrim, 4):
        copy.start()
    gather_faces(3)
    change1[...] = change()
    for copy in pair(wout, wrim, 4):
        copy.wait_recv()
    low, high_rim = rims(wrim)
    far_w = jnp.concatenate([x[:, 256 * l:256 * l + 256] for x in (low, high_rim) for l in range(4)], axis=0)
    wh, wl = split(jnp.concatenate([own_w, far_w], axis=0))
    got = dot(jnp.concatenate([wh, wl], axis=0), hot[...])
    got = got[0:16] + got[16:32]
    near = []
    for k in range(4):
        mine = iota((16, ELEMS), 0) == (nel_ref[k:k + 1, :] >> 8)
        near_w = jnp.sum(jnp.where(mine, got[:, ELEMS * k:ELEMS * k + ELEMS], 0.0), axis=0, keepdims=True)
        near.append(jnp.where(iota((4, ELEMS), 0) == nfa_ref[k:k + 1, :], near_w, 0.0))
    near.append(w)
    near.append(jnp.zeros((128 - 17, ELEMS), F32))
    nh, nl = split(jnp.concatenate(near, axis=0))
    first = dot(uu[...], nh)
    extra = first[0:QP] + first[QB:QB + QP] + dot(uu[0:QB, :], nl)[0:QP]
    result = s1[...] + push * w + scale * (change1[...] + extra)
    new_state_ref[...] = result[0:Q]

    for index, (outs, ins) in enumerate(((out1, rim1), (out2, rim2), (wout, wrim))):
        for copy in pair(outs, ins, 2 * index):
            copy.wait_send()
    for copy in edges(0) + edges(1):
        copy.wait_send()
    sent_all(cells_out, cells_in, cell_send, cell_recv)
    sent_all(open_out, open_in, open_send, open_recv)
    sent_all(press_out, press_in, pr_send, pr_recv)


def interleaved(x):
    return x.reshape(2, 64, 128).transpose(1, 0, 2).reshape(128, 128)


def straight(x):
    return x.reshape(64, 2, 128).transpose(1, 0, 2).reshape(1, 2, 8192)


def shards(
    rock_state, jacobian, stiffness, trace_map, lift_map, neighbor_elem, neighbor_face, send_elem,
    opening_dir, traction_dir, face_elem, face_tile, face_cell, face_count, pressure, base_aperture, injection,
):
    vmem = pl.BlockSpec(memory_space=pltpu.VMEM)
    smem = pl.BlockSpec(memory_space=pltpu.SMEM)
    scratch = [
        pltpu.VMEM((QP, ELEMS), F32),
        pltpu.VMEM((640, 512), BF16),
        pltpu.VMEM((256, SLOTS), BF16),
        pltpu.VMEM((256, 2 * HALO), BF16),
        pltpu.VMEM((256, ELEMS), BF16),
        pltpu.VMEM((256, ELEMS), BF16),
        pltpu.VMEM((2 * QB, 256), BF16),
        pltpu.VMEM((2 * QB, QB), BF16),
        pltpu.VMEM((2 * QB, 128), BF16),
        pltpu.VMEM((2, QP, HALO), F32),
        pltpu.VMEM((2, QP, HALO), F32),
        pltpu.VMEM((2, QP, HALO), F32),
        pltpu.VMEM((2, QP, HALO), F32),
        pltpu.VMEM((2, 1, HALO), F32),
        pltpu.VMEM((2, 1, HALO), F32),
        pltpu.VMEM((256, SLOTS), BF16),
        pltpu.VMEM((256, SLOTS), BF16),
        pltpu.VMEM((128, SLOTS), BF16),
        pltpu.VMEM((2, 64, 128), F32),
        pltpu.VMEM((TILES, 4, 128), F32),
        pltpu.VMEM((TILES, 4, 128), F32),
        pltpu.VMEM((TILES, 4, 128), F32),
        pltpu.VMEM((TILES, 4, 128), F32),
        pltpu.VMEM((TILES, 4, 128), F32),
        pltpu.VMEM((TILES, 4, 128), F32),
        pltpu.VMEM((6, 64, 128), I32),
        pltpu.VMEM((128, SLOTS), BF16),
        pltpu.VMEM((128, SLOTS), BF16),
        pltpu.VMEM((128, SLOTS), F32),
        pltpu.VMEM((128, 128), F32),
        pltpu.VMEM((4, 64, 128), F32),
        pltpu.VMEM((4, 64, 128), F32),
        pltpu.VMEM((2, 128, 128), F32),
        pltpu.VMEM((QP, ELEMS), F32),
        pltpu.VMEM((1, ELEMS), F32),
    ] + [pltpu.SemaphoreType.DMA((n,)) for n in (6, 6, 15, 15, 15, 15, 15, 15, 4, 4)]
    new_state, new_pressure, aperture = pl.pallas_call(
        kernel,
        out_shape=(
            jax.ShapeDtypeStruct((Q, ELEMS), F32),
            jax.ShapeDtypeStruct((128, 128), F32),
            jax.ShapeDtypeStruct((128, 128), F32),
        ),
        in_specs=[vmem] * 13 + [smem] + [vmem] * 3,
        out_specs=(vmem,) * 3,
        scratch_shapes=scratch,
        compiler_params=pltpu.CompilerParams(
            collective_id=0, has_side_effects=True, vmem_limit_bytes=56 * 2**20),
    )(
        rock_state, jacobian.reshape(1, ELEMS), stiffness, trace_map, lift_map, neighbor_elem, neighbor_face,
        send_elem, opening_dir.reshape(1, Q), traction_dir.reshape(1, Q), face_elem.reshape(64, 128),
        face_tile.reshape(64, 128), face_cell.reshape(64, 128), face_count, interleaved(pressure),
        interleaved(base_aperture), interleaved(injection),
    )
    return new_state, straight(new_pressure), straight(aperture)


def solution(mesh):
    elems = P(None, ("rock", "plane"))
    flat = P(("rock", "plane"))
    grid = P("rock", "plane", None)
    return jax.shard_map(
        shards,
        mesh=mesh,
        in_specs=(elems, flat, P(), P(), P(), elems, elems, elems, P(), P(), flat, flat, flat, flat, grid, grid, grid),
        out_specs=(elems, grid, grid),
        check_vma=False,
    )
```

```python
import jax
import jax.numpy as jnp
from jax import lax
from jax.experimental import pallas as pl
from jax.experimental.pallas import tpu as pltpu
from jax.sharding import PartitionSpec as P

STEP = 0.25
RATE = 0.35
F32 = jnp.float32
BF16 = jnp.bfloat16
I32 = jnp.int32
MESH = pl.DeviceIdType.MESH
Q = 36
QP = 40
QB = 48
ELEMS = 2048
HALO = 1024
SLOTS = 8192
TILES = 16
PARTS = 128


def dot(a, b):
    return jnp.dot(a, b, preferred_element_type=F32)


def dot_nt(a, b):
    return lax.dot_general(a, b, (((1,), (1,)), ((), ())), preferred_element_type=F32)


def exact_dot(a, b):
    return jnp.dot(a, b, preferred_element_type=F32, precision=lax.Precision.HIGHEST)


def split(x):
    high = x.astype(BF16)
    return high, (x - high.astype(F32)).astype(BF16)


def iota(shape, dim):
    return lax.broadcasted_iota(I32, shape, dim)


def ones_where(mask):
    return jnp.where(mask, 1.0, 0.0).astype(F32)


def units(count, row):
    return ones_where(iota((count, row.shape[1]), 0) == row).astype(BF16)


def lanes(chunk, width=128):
    return pl.ds(pl.multiple_of(chunk * width, width), width)


def padded(x, rows):
    return jnp.concatenate([x, jnp.zeros((rows - x.shape[0],) + x.shape[1:], x.dtype)], axis=0)


def column(row):
    wide = jnp.broadcast_to(row, (QP, Q))
    eye = iota((QP, Q), 0) == iota((QP, Q), 1)
    return jnp.sum(jnp.where(eye, wide, 0.0), axis=1, keepdims=True)


def kernel(
    state_hbm, jac_hbm, stiff_hbm, tmap_hbm, lift_hbm, nel_hbm, nfa_hbm, send_hbm, odir_hbm, tdir_hbm,
    fel_hbm, ftile_hbm, fcell_hbm, fcount_ref, press_hbm, base_hbm, inj_hbm,
    new_state_ref, new_press_ref, aper_ref,
    s1, table, hot, send_hot, xh, xl, ww, tw, uu, gw, gtab, out1, out2, rim1, rim2, wout, wrim,
    elem_hot, elem_hi, elem_lo, cells_out, cells_in, open_out, open_in, press_out, press_in,
    slot_tab, cell_hot, cell_unit, cell_row, cond, edge_out, edge_in, edge_wide, own2, lane_row, slot_row,
    state_ref, jac_ref, stiff_ref, tmap_ref, lift_ref, nel_ref, nfa_ref, send_ref, odir_ref, tdir_ref,
    fel_ref, ftile_ref, fcell_ref, press_ref, base_ref, inj_ref, in_sem,
    halo_send, halo_recv, cell_send, cell_recv, open_send, open_recv, pr_send, pr_recv, edge_send, edge_recv,
):
    loads = [
        pltpu.make_async_copy(source, target, in_sem.at[i])
        for i, (source, target) in enumerate((
            (state_hbm, state_ref), (tmap_hbm, tmap_ref), (send_hbm, send_ref), (lift_hbm, lift_ref),
            (ftile_hbm, ftile_ref), (fcell_hbm, fcell_ref), (fel_hbm, fel_ref), (press_hbm, press_ref),
            (nel_hbm, nel_ref), (nfa_hbm, nfa_ref), (stiff_hbm, stiff_ref), (odir_hbm, odir_ref),
            (jac_hbm, jac_ref), (tdir_hbm, tdir_ref), (base_hbm, base_ref), (inj_hbm, inj_ref)))
    ]
    for load in loads[:4]:
        load.start()
    rock = lax.axis_index("rock")
    plane = lax.axis_index("plane")
    here = rock * TILES + plane
    nxt = lax.rem(here + 1, PARTS)
    prv = lax.rem(here + PARTS - 1, PARTS)
    next_part = (lax.div(nxt, TILES), lax.rem(nxt, TILES))
    prev_part = (lax.div(prv, TILES), lax.rem(prv, TILES))
    next_tile = (rock, lax.rem(plane + 1, TILES))
    prev_tile = (rock, lax.rem(plane + TILES - 1, TILES))

    def peer(o):
        return lax.rem(plane + o, TILES)

    barrier = pltpu.get_barrier_semaphore()
    for target in (next_part, prev_part):
        pl.semaphore_signal(barrier, inc=1, device_id=target, device_id_type=MESH)

    def greet(o, carry):
        pl.semaphore_signal(barrier, inc=1, device_id=(rock, peer(o)), device_id_type=MESH)
        return carry

    lax.fori_loop(1, TILES, greet, 0)
    for load in loads[4:]:
        load.start()

    def pair(outs, ins, index):
        return [
            pltpu.make_async_remote_copy(
                outs.at[0], ins.at[1], halo_send.at[index], halo_recv.at[index],
                device_id=prev_part, device_id_type=MESH),
            pltpu.make_async_remote_copy(
                outs.at[1], ins.at[0], halo_send.at[index + 1], halo_recv.at[index + 1],
                device_id=next_part, device_id_type=MESH),
        ]

    def edges(index):
        return [
            pltpu.make_async_remote_copy(
                edge_out.at[2 * index], edge_in.at[2 * index + 1], edge_send.at[2 * index],
                edge_recv.at[2 * index], device_id=prev_tile, device_id_type=MESH),
            pltpu.make_async_remote_copy(
                edge_out.at[2 * index + 1], edge_in.at[2 * index], edge_send.at[2 * index + 1],
                edge_recv.at[2 * index + 1], device_id=next_tile, device_id_type=MESH),
        ]

    def swap(outs, ins, sends, recvs, o):
        return pltpu.make_async_remote_copy(
            outs.at[peer(o)], ins.at[plane], sends.at[o - 1], recvs.at[o - 1],
            device_id=(rock, peer(o)), device_id_type=MESH)

    def start_all(*what):
        def one(o, carry):
            swap(*what, o).start()
            return carry
        lax.fori_loop(1, TILES, one, 0)
        outs, ins = what[:2]
        ins[plane] = outs[plane]

    def arrive_all(*what):
        def one(o, carry):
            swap(*what, o).wait_recv()
            return carry
        lax.fori_loop(1, TILES, one, 0)

    def sent_all(*what):
        def one(o, carry):
            swap(*what, o).wait_send()
            return carry
        lax.fori_loop(1, TILES, one, 0)

    for load in loads[:4]:
        load.wait()
    tmap = tmap_ref[...]
    lift = lift_ref[...]
    widen = ones_where(iota((Q, QB), 0) == iota((Q, QB), 1)).astype(BF16)
    th, tl = split(padded(tmap, QB))
    tw[0:QB, :] = dot(th, widen).astype(BF16)
    tw[QB:2 * QB, :] = dot(tl, widen).astype(BF16)

    def put_state(x):
        high, rest = split(padded(x, QB))
        xh[0:QB, :] = high
        xl[0:QB, :] = rest

    def traces():
        first = dot(tw[...], xh[0:QB, :])
        return first[0:QP] + first[QB:QB + QP] + dot(tw[0:QB, :], xl[0:QB, :])[0:QP]

    def put_table(parts, start):
        rows = jnp.concatenate(
            [x[:, 256 * l:256 * l + 256] for x in parts for l in range(x.shape[1] // 256)], axis=0)
        high, rest = split(rows)
        table[start:start + rows.shape[0], 0:256] = high
        table[start:start + rows.shape[0], 256:512] = rest

    def pick(got, rows, which, first, count):
        for l in range(count):
            part = rows[QP * l:QP * l + QP]
            got = part if got is None else jnp.where(which == first + l, part, got)
        return got

    def fill_outgoing(out):
        for side in range(2):
            a = send_hot[:, HALO * side:HALO * side + HALO]
            rows = dot(table[0:320, :], jnp.concatenate([a, a], axis=0))
            out[side] = pick(None, rows, send_ref[side:side + 1, :] >> 8, 0, 8)

    def rims(rim):
        lower = jnp.where(here > 0, rim[0], 0.0)
        upper = jnp.where(here < PARTS - 1, rim[1], 0.0)
        return lower, upper

    face_of_row = lax.div(iota((QP, 1), 0), 9)

    def columns(k, rows):
        a = hot[:, ELEMS * k:ELEMS * k + ELEMS]
        return dot(rows, jnp.concatenate([a, a], axis=0))

    def put_faces(k, got):
        got = jnp.where(face_of_row == nfa_ref[k:k + 1, :], got, 0.0)
        high, rest = split(padded(got, QB))
        xh[QB * (k + 1):QB * (k + 2), :] = high
        xl[QB * (k + 1):QB * (k + 2), :] = rest

    def gather_faces(k):
        put_faces(k, pick(None, columns(k, table[...]), nel_ref[k:k + 1, :] >> 8, 0, 16))

    def gather_own(k):
        own2[k] = pick(None, columns(k, table[0:320, :]), nel_ref[k:k + 1, :] >> 8, 0, 8)

    def gather_rims(k):
        put_faces(k, pick(own2[k], columns(k, table[320:640, :]), nel_ref[k:k + 1, :] >> 8, 8, 8))

    def change():
        first = dot(ww[...], xh[...])
        return first[0:QP] + first[QB:QB + QP] + dot(ww[0:QB, :], xl[...])[0:QP]

    s1[0:Q, :] = state_ref[...]
    s1[Q:QP, :] = jnp.zeros((QP - Q, ELEMS), F32)
    put_state(s1[...])
    tr = traces()
    put_table([tr], 0)

    for side in range(2):
        send_hot[:, HALO * side:HALO * side + HALO] = units(256, send_ref[side:side + 1, :] & 255)
    fill_outgoing(out1)
    pl.semaphore_wait(barrier, TILES + 1)
    for copy in pair(out1, rim1, 0):
        copy.start()
    for load in loads[4:]:
        load.wait()
    edge_out[0] = press_ref[pl.ds(0, 64, stride=2), :]
    edge_out[1] = press_ref[pl.ds(1, 64, stride=2), :]
    for copy in edges(0):
        copy.start()

    tile = ftile_ref[...]
    upper = ones_where(iota((128, 128), 0) <= iota((128, 128), 1)).astype(BF16)
    count = jnp.concatenate([upper, jnp.ones((128, 128), BF16)], axis=0)
    before = ones_where(iota((64, 64), 1) < iota((64, 64), 0)).astype(BF16)
    named = [ones_where(tile == t).astype(BF16) for t in range(TILES)]
    earlier = dot(before, jnp.concatenate(named, axis=1)).astype(BF16)
    ranks = dot(
        jnp.concatenate(
            [jnp.concatenate([named[t], earlier[:, 128 * t:128 * t + 128]], axis=1) for t in range(TILES)],
            axis=0),
        count)
    place = jnp.zeros((64, 128), F32)
    for t in range(TILES):
        place = jnp.where(tile == t, ranks[64 * t:64 * t + 64] + (512.0 * t - 1.0), place)
    place = place.astype(I32)
    cell = fcell_ref[...]
    elem = fel_ref[...]
    row = ((cell >> 7) & 63) * 2 + (cell >> 13)
    code = (row & 63) * 256 + (row >> 6) * 128 + (cell & 127)
    slot = iota((64, 128), 0) * 128 + iota((64, 128), 1)
    live = jnp.where(slot < fcount_ref[0], 128, 0)
    slot_tab[0] = (place >> 7).astype(F32)
    slot_tab[1] = (place & 127).astype(F32)
    slot_tab[2] = ((code >> 5) - 256).astype(F32)
    slot_tab[3] = ((code & 31) * 16 + (elem >> 7) - 256).astype(F32)
    slot_tab[4] = ((elem & 127) + live).astype(F32)

    row64 = iota((64, 128), 0).astype(F32)
    row128 = iota((128, 128), 0).astype(F32)

    def order_body(half, total):
        named = []
        inner = []
        for u in range(32):
            at = pl.ds(32 * half + u, 1)
            mine = row64 == slot_tab[0, at, :]
            named.append(jnp.concatenate(
                [jnp.where(mine, slot_tab[2 + v, at, :], 0.0).astype(BF16) for v in range(3)], axis=0))
            inner.append(ones_where(row128 == slot_tab[1, at, :]).astype(BF16))
        return total + dot_nt(jnp.concatenate(named, axis=1), jnp.concatenate(inner, axis=1))

    grouped = lax.fori_loop(0, 2, order_body, jnp.zeros((192, 128), F32)).astype(I32)
    middle = grouped[64:128] + 256
    code = ((grouped[0:64] + 256) * 32 + (middle >> 4)).astype(F32)
    high = ((middle & 15) + ((grouped[128:192] >> 7) << 4)).astype(F32)
    low = (grouped[128:192] & 127).astype(F32)
    for c in range(64):
        at = slice(128 * c, 128 * c + 128)
        inner = slice(128 * (c % 4), 128 * (c % 4) + 128)
        cells_out[c // 4, :, inner] = code[c:c + 1]
        elem_hi[:, at] = high[c:c + 1]
        elem_lo[:, at] = low[c:c + 1]
    start_all(cells_out, cells_in, cell_send, cell_recv)

    for k in range(4):
        hot[:, ELEMS * k:ELEMS * k + ELEMS] = units(256, nel_ref[k:k + 1, :] & 255)

    for k in range(4):
        at = slice(2048 * k, 2048 * k + 2048)
        elem_hot[:, at] = units(128, elem_lo[:, at].astype(I32))

    volume = stiff_ref[...] - exact_dot(lift, tmap)
    same = ones_where(lax.rem(iota((Q, Q), 0), 9) == lax.rem(iota((Q, Q), 1), 9))
    odir = odir_ref[...]
    of_face = jnp.where(lax.div(iota((16, Q), 0), 4) == lax.div(iota((16, Q), 1), 9), exact_dot(odir, lift), 0.0)
    of_face = exact_dot(of_face, same)
    gh, gl = split(jnp.where(lax.rem(iota((16, Q), 0), 4) == lax.div(iota((16, Q), 1), 9), of_face, 0.0))
    gw[0:16, :] = dot(gh, widen).astype(BF16)
    gw[16:32, :] = dot(gl, widen).astype(BF16)

    def put_scores(parts, start):
        for x in parts:
            high, rest = split(padded(x, QB))
            got = dot(gw[...], high)
            got = got[0:16] + got[16:32] + dot(gw[0:16, :], rest)
            for l in range(x.shape[1] // 256):
                for half in range(2):
                    at = 256 * l + 128 * half
                    gtab[half, pl.ds(start + l, 16, stride=16), :] = got[:, at:at + 128]
            start += x.shape[1] // 256

    put_scores([tr], 0)
    scale = STEP * jac_ref[...]
    own_state = s1[...]
    direct = jnp.sum(column(odir) * own_state, axis=0, keepdims=True)
    within = jnp.sum(column(exact_dot(odir, volume)) * own_state, axis=0, keepdims=True)

    for copy in pair(out1, rim1, 0):
        copy.wait_recv()
    put_scores(rims(rim1), 8)
    for k in range(4):
        at = slice(64 * k, 64 * k + 64)
        gh, gl = split(jnp.concatenate([gtab[0, at, :], gtab[1, at, :]], axis=1))
        got = dot(jnp.concatenate([gh, gl], axis=0), hot[:, ELEMS * k:ELEMS * k + ELEMS])
        mine = iota((64, ELEMS), 0) == nfa_ref[k:k + 1, :] * 16 + (nel_ref[k:k + 1, :] >> 8)
        within = within + jnp.sum(jnp.where(mine, got[0:64] + got[64:128], 0.0), axis=0, keepdims=True)
    score = direct + scale * within

    opening = 0.2 * (jnp.maximum(score, 0.0) + jnp.log1p(jnp.exp(-jnp.abs(score))))
    oh, ol = split(jnp.concatenate([opening[:, 128 * i:128 * i + 128] for i in range(16)], axis=0))
    got = dot(jnp.concatenate([oh, ol], axis=0), elem_hot[...])
    sixteen = (iota((16, 1), 0) + 16).astype(F32)
    picked = jnp.sum(
        jnp.where(sixteen == elem_hi[...], got[0:16] + got[16:32], 0.0), axis=0, keepdims=True)
    for t in range(TILES):
        open_out[t] = picked[:, 512 * t:512 * t + 512]
    start_all(open_out, open_in, open_send, open_recv)

    arrive_all(cells_out, cells_in, cell_send, cell_recv)

    for t in range(TILES):
        at = slice(512 * t, 512 * t + 512)
        where = cells_in[t].astype(I32)
        cell_hot[:, at] = units(256, where & 255)
        cell_unit[:, at] = units(64, where >> 8)
        cell_row[:, at] = where >> 8

    row_i = iota((Q, 256), 0)
    col_i = iota((Q, 256), 1)
    own_block = ones_where(row_i == col_i).astype(BF16)
    blk = lax.div(col_i, QB)
    inner = lax.rem(col_i, QB)
    face_block = ones_where(
        (blk >= 1) & (blk <= 4) & (inner < Q) & (row_i == 9 * (blk - 1) + lax.rem(inner, 9))).astype(BF16)
    mh, ml = split(padded(volume, QB))
    lh, ll = split(padded(lift, QB))
    ww[0:QB, :] = (dot(mh, own_block) + dot(lh, face_block)).astype(BF16)
    ww[QB:2 * QB, :] = (dot(ml, own_block) + dot(ll, face_block)).astype(BF16)
    xh[5 * QB:256, :] = jnp.zeros((16, ELEMS), BF16)
    xl[5 * QB:256, :] = jnp.zeros((16, ELEMS), BF16)
    put_table(list(rims(rim1)), 320)
    gather_faces(0)
    gather_faces(1)

    arrive_all(open_out, open_in, open_send, open_recv)

    amounts = []
    for t in range(TILES):
        high = open_in[t].astype(BF16).astype(F32)
        unit = cell_unit[:, 512 * t:512 * t + 512]
        amounts.append(jnp.concatenate(
            [unit * jnp.concatenate([jnp.broadcast_to(part, (16, 512)).astype(BF16)] * 4, axis=0)
             for part in (high, open_in[t] - high)], axis=0))
    field = dot_nt(jnp.concatenate(amounts, axis=1), cell_hot[...])
    field = field[0:64] + field[64:128]
    aper = base_ref[...] + jnp.concatenate([field[:, 0:128], field[:, 128:256]], axis=0)
    aper_ref[...] = aper
    c = aper * aper * aper / 12.0
    cond[...] = c
    edge_out[2] = cond[pl.ds(0, 64, stride=2), :]
    edge_out[3] = cond[pl.ds(1, 64, stride=2), :]
    for copy in edges(1):
        copy.start()

    gather_faces(2)
    gather_faces(3)
    s1[...] = s1[...] + scale * change()

    put_state(s1[...])
    put_table([traces()], 0)
    fill_outgoing(out2)
    for copy in pair(out2, rim2, 2):
        copy.start()
    p = press_ref[...]
    odd = (iota((128, 128), 0) & 1) == 1
    lane = iota((128, 128), 1)
    block = iota((128, 128), 0) >> 1
    for copy in edges(0) + edges(1):
        copy.wait_recv()
    for i in range(2):
        edge_wide[i, pl.ds(0, 64, stride=2), :] = edge_in[2 * i]
        edge_wide[i, pl.ds(1, 64, stride=2), :] = edge_in[2 * i + 1]

    def sides(x, wide):
        after = pltpu.roll(x, 127, 1)
        after = jnp.where(lane == 127, pltpu.roll(after, 126, 0), after)
        ahead = pltpu.roll(x, 1, 1)
        ahead = jnp.where(lane == 0, pltpu.roll(ahead, 2, 0), ahead)
        up = jnp.where(odd, pltpu.roll(x, 1, 0), wide)
        down = jnp.where(odd, wide, pltpu.roll(x, 127, 0))
        inside = (
            (lane < 127) | (block < 63),
            (lane > 0) | (block > 0),
            odd | (plane > 0),
            jnp.logical_not(odd) | (plane < TILES - 1),
        )
        return [jnp.where(m, v, 0.0) for m, v in zip(inside, (after, ahead, up, down))]

    inflow = jnp.zeros((128, 128), F32)
    for other_p, other_c in zip(sides(p, edge_wide[0]), sides(c, edge_wide[1])):
        inflow = inflow + 2.0 * c * other_c / (c + other_c) * (other_p - p)
    new_p = p + RATE * (inflow + inj_ref[...])
    new_press_ref[...] = new_p

    ph, prest = split(jnp.concatenate([new_p[0:64], new_p[64:128]], axis=1))
    pressures = jnp.concatenate([ph, prest], axis=0)
    for b in range(4):
        at = slice(2048 * b, 2048 * b + 2048)
        got = dot(pressures, cell_hot[:, at])
        mine = iota((64, 2048), 0) == cell_row[:, at]
        picked = jnp.sum(jnp.where(mine, got[0:64] + got[64:128], 0.0), axis=0, keepdims=True)
        for t in range(4):
            press_out[4 * b + t] = picked[:, 512 * t:512 * t + 512]
    start_all(press_out, press_in, pr_send, pr_recv)

    for k in range(4):
        gather_own(k)

    push = column(tdir_ref[...])
    tau = exact_dot(tmap, push[0:Q])
    of_facet = jnp.where(lax.div(iota((Q, 128), 0), 9) == lax.rem(iota((Q, 128), 1), 4), tau, 0.0)
    spread = jnp.where(
        lax.div(iota((Q, 128), 0), 9) == lax.div(iota((Q, 128), 1), 4), exact_dot(same, of_facet), 0.0)
    load_map = jnp.where(
        iota((Q, 128), 1) == 16, exact_dot(volume, push[0:Q]), exact_dot(lift, spread))
    uh, ul = split(padded(load_map, QB))
    uu[0:QB, :] = uh
    uu[QB:2 * QB, :] = ul
    arrive_all(press_out, press_in, pr_send, pr_recv)

    for t in range(TILES):
        slot_row[:, 512 * t:512 * t + 512] = press_in[t]
    high, rest = split(jnp.where(sixteen == elem_hi[...], slot_row[...], 0.0))
    load = dot_nt(jnp.concatenate([high, rest], axis=0), elem_hot[...])
    load = load[0:16] + load[16:32]
    for i in range(16):
        lane_row[:, 128 * i:128 * i + 128] = load[i:i + 1]
    w = scale * lane_row[...]
    own_w = jnp.concatenate([w[:, 256 * l:256 * l + 256] for l in range(8)], axis=0)
    wh, wl = split(own_w)
    got = dot(jnp.concatenate([wh, wl], axis=0), send_hot[...])
    got = got[0:8] + got[8:16]
    for side in range(2):
        mine = iota((8, HALO), 0) == (send_ref[side:side + 1, :] >> 8)
        wout[side] = jnp.sum(
            jnp.where(mine, got[:, HALO * side:HALO * side + HALO], 0.0), axis=0, keepdims=True)
    for copy in pair(wout, wrim, 4):
        copy.start()
    for copy in pair(out2, rim2, 2):
        copy.wait_recv()
    put_table(list(rims(rim2)), 320)
    for k in range(4):
        gather_rims(k)
    change2 = change()
    for copy in pair(wout, wrim, 4):
        copy.wait_recv()
    low, high_rim = rims(wrim)
    far_w = jnp.concatenate([x[:, 256 * l:256 * l + 256] for x in (low, high_rim) for l in range(4)], axis=0)
    wh, wl = split(jnp.concatenate([own_w, far_w], axis=0))
    got = dot(jnp.concatenate([wh, wl], axis=0), hot[...])
    got = got[0:16] + got[16:32]
    near = []
    for k in range(4):
        mine = iota((16, ELEMS), 0) == (nel_ref[k:k + 1, :] >> 8)
        near_w = jnp.sum(jnp.where(mine, got[:, ELEMS * k:ELEMS * k + ELEMS], 0.0), axis=0, keepdims=True)
        near.append(jnp.where(iota((4, ELEMS), 0) == nfa_ref[k:k + 1, :], near_w, 0.0))
    near.append(w)
    near.append(jnp.zeros((128 - 17, ELEMS), F32))
    nh, nl = split(jnp.concatenate(near, axis=0))
    first = dot(uu[...], nh)
    extra = first[0:QP] + first[QB:QB + QP] + dot(uu[0:QB, :], nl)[0:QP]
    result = s1[...] + push * w + scale * (change2 + extra)
    new_state_ref[...] = result[0:Q]

    for index, (outs, ins) in enumerate(((out1, rim1), (out2, rim2), (wout, wrim))):
        for copy in pair(outs, ins, 2 * index):
            copy.wait_send()
    for copy in edges(0) + edges(1):
        copy.wait_send()
    sent_all(cells_out, cells_in, cell_send, cell_recv)
    sent_all(open_out, open_in, open_send, open_recv)
    sent_all(press_out, press_in, pr_send, pr_recv)


def interleaved(x):
    return x.reshape(2, 64, 128).transpose(1, 0, 2).reshape(128, 128)


def straight(x):
    return x.reshape(64, 2, 128).transpose(1, 0, 2).reshape(1, 2, 8192)


def shards(
    rock_state, jacobian, stiffness, trace_map, lift_map, neighbor_elem, neighbor_face, send_elem,
    opening_dir, traction_dir, face_elem, face_tile, face_cell, face_count, pressure, base_aperture, injection,
):
    vmem = pl.BlockSpec(memory_space=pltpu.VMEM)
    hbm = pl.BlockSpec(memory_space=pltpu.HBM)
    smem = pl.BlockSpec(memory_space=pltpu.SMEM)
    scratch = [
        pltpu.VMEM((QP, ELEMS), F32),
        pltpu.VMEM((640, 512), BF16),
        pltpu.VMEM((256, SLOTS), BF16),
        pltpu.VMEM((256, 2 * HALO), BF16),
        pltpu.VMEM((256, ELEMS), BF16),
        pltpu.VMEM((256, ELEMS), BF16),
        pltpu.VMEM((2 * QB, 256), BF16),
        pltpu.VMEM((2 * QB, QB), BF16),
        pltpu.VMEM((2 * QB, 128), BF16),
        pltpu.VMEM((32, QB), BF16),
        pltpu.VMEM((2, 256, 128), F32),
        pltpu.VMEM((2, QP, HALO), F32),
        pltpu.VMEM((2, QP, HALO), F32),
        pltpu.VMEM((2, QP, HALO), F32),
        pltpu.VMEM((2, QP, HALO), F32),
        pltpu.VMEM((2, 1, HALO), F32),
        pltpu.VMEM((2, 1, HALO), F32),
        pltpu.VMEM((128, SLOTS), BF16),
        pltpu.VMEM((1, SLOTS), F32),
        pltpu.VMEM((1, SLOTS), F32),
        pltpu.VMEM((TILES, 1, 512), F32),
        pltpu.VMEM((TILES, 1, 512), F32),
        pltpu.VMEM((TILES, 1, 512), F32),
        pltpu.VMEM((TILES, 1, 512), F32),
        pltpu.VMEM((TILES, 1, 512), F32),
        pltpu.VMEM((TILES, 1, 512), F32),
        pltpu.VMEM((5, 64, 128), F32),
        pltpu.VMEM((256, SLOTS), BF16),
        pltpu.VMEM((64, SLOTS), BF16),
        pltpu.VMEM((1, SLOTS), I32),
        pltpu.VMEM((128, 128), F32),
        pltpu.VMEM((4, 64, 128), F32),
        pltpu.VMEM((4, 64, 128), F32),
        pltpu.VMEM((2, 128, 128), F32),
        pltpu.VMEM((4, QP, ELEMS), F32),
        pltpu.VMEM((1, ELEMS), F32),
        pltpu.VMEM((1, SLOTS), F32),
        pltpu.VMEM((Q, ELEMS), F32),
        pltpu.VMEM((1, ELEMS), F32),
        pltpu.VMEM((Q, Q), F32),
        pltpu.VMEM((Q, Q), F32),
        pltpu.VMEM((Q, Q), F32),
        pltpu.VMEM((4, ELEMS), I32),
        pltpu.VMEM((4, ELEMS), I32),
        pltpu.VMEM((2, HALO), I32),
        pltpu.VMEM((1, Q), F32),
        pltpu.VMEM((1, Q), F32),
        pltpu.VMEM((64, 128), I32),
        pltpu.VMEM((64, 128), I32),
        pltpu.VMEM((64, 128), I32),
        pltpu.VMEM((128, 128), F32),
        pltpu.VMEM((128, 128), F32),
        pltpu.VMEM((128, 128), F32),
    ] + [pltpu.SemaphoreType.DMA((n,)) for n in (16, 6, 6, 15, 15, 15, 15, 15, 15, 4, 4)]
    new_state, new_pressure, aperture = pl.pallas_call(
        kernel,
        out_shape=(
            jax.ShapeDtypeStruct((Q, ELEMS), F32),
            jax.ShapeDtypeStruct((128, 128), F32),
            jax.ShapeDtypeStruct((128, 128), F32),
        ),
        in_specs=[hbm] * 13 + [smem] + [hbm] * 3,
        out_specs=(vmem,) * 3,
        scratch_shapes=scratch,
        compiler_params=pltpu.CompilerParams(
            collective_id=0, has_side_effects=True, vmem_limit_bytes=56 * 2**20),
    )(
        rock_state, jacobian.reshape(1, ELEMS), stiffness, trace_map, lift_map, neighbor_elem, neighbor_face,
        send_elem, opening_dir.reshape(1, Q), traction_dir.reshape(1, Q), face_elem.reshape(64, 128),
        face_tile.reshape(64, 128), face_cell.reshape(64, 128), face_count, interleaved(pressure),
        interleaved(base_aperture), interleaved(injection),
    )
    return new_state, straight(new_pressure), straight(aperture)


def solution(mesh):
    elems = P(None, ("rock", "plane"))
    flat = P(("rock", "plane"))
    grid = P("rock", "plane", None)
    return jax.shard_map(
        shards,
        mesh=mesh,
        in_specs=(elems, flat, P(), P(), P(), elems, elems, elems, P(), P(), flat, flat, flat, flat, grid, grid, grid),
        out_specs=(elems, grid, grid),
        check_vma=False,
    )
```

```python
import jax
import jax.numpy as jnp
from jax import lax
from jax.experimental import pallas as pl
from jax.experimental.pallas import tpu as pltpu
from jax.sharding import PartitionSpec as P

STEP = 0.25
RATE = 0.35
F32 = jnp.float32
BF16 = jnp.bfloat16
I32 = jnp.int32
MESH = pl.DeviceIdType.MESH
Q = 36
QP = 40
QB = 48
ELEMS = 2048
HALO = 1024
SLOTS = 8192
TILES = 16
PARTS = 128


def dot(a, b):
    return jnp.dot(a, b, preferred_element_type=F32)


def dot_nt(a, b):
    return lax.dot_general(a, b, (((1,), (1,)), ((), ())), preferred_element_type=F32)


def exact_dot(a, b):
    return jnp.dot(a, b, preferred_element_type=F32, precision=lax.Precision.HIGHEST)


def split(x):
    high = x.astype(BF16)
    return high, (x - high.astype(F32)).astype(BF16)


def iota(shape, dim):
    return lax.broadcasted_iota(I32, shape, dim)


def ones_where(mask):
    return jnp.where(mask, 1.0, 0.0).astype(F32)


def units(count, row):
    return ones_where(iota((count, row.shape[1]), 0) == row).astype(BF16)


def lanes(chunk, width=128):
    return pl.ds(pl.multiple_of(chunk * width, width), width)


def padded(x, rows):
    return jnp.concatenate([x, jnp.zeros((rows - x.shape[0],) + x.shape[1:], x.dtype)], axis=0)


def column(row):
    wide = jnp.broadcast_to(row, (QP, Q))
    eye = iota((QP, Q), 0) == iota((QP, Q), 1)
    return jnp.sum(jnp.where(eye, wide, 0.0), axis=1, keepdims=True)


def kernel(
    state_hbm, jac_hbm, stiff_hbm, tmap_hbm, lift_hbm, nel_hbm, nfa_hbm, send_hbm, odir_hbm, tdir_hbm,
    fel_hbm, ftile_hbm, fcell_hbm, fcount_ref, press_hbm, base_hbm, inj_hbm,
    new_state_ref, new_press_ref, aper_ref,
    s1, table, hot, send_hot, xh, xl, ww, tw, uu, gw, gtab, out1, out2, rim1, rim2, wout, wrim, gout, grim,
    elem_hot, elem_hi, elem_lo, cells_out, cells_in, open_out, open_in, press_out, press_in,
    slot_tab, cell_hot, cell_unit, cell_row, cond, edge_out, edge_in, edge_wide, own2, lane_row, slot_row,
    state_ref, jac_ref, stiff_ref, tmap_ref, lift_ref, nel_ref, nfa_ref, send_ref, odir_ref, tdir_ref,
    fel_ref, ftile_ref, fcell_ref, press_ref, base_ref, inj_ref, in_sem,
    halo_send, halo_recv, cell_send, cell_recv, open_send, open_recv, pr_send, pr_recv, edge_send, edge_recv,
):
    loads = [
        pltpu.make_async_copy(source, target, in_sem.at[i])
        for i, (source, target) in enumerate((
            (state_hbm, state_ref), (tmap_hbm, tmap_ref), (send_hbm, send_ref), (lift_hbm, lift_ref),
            (odir_hbm, odir_ref), (ftile_hbm, ftile_ref), (fcell_hbm, fcell_ref), (fel_hbm, fel_ref), (press_hbm, press_ref),
            (nel_hbm, nel_ref), (nfa_hbm, nfa_ref), (stiff_hbm, stiff_ref),
            (jac_hbm, jac_ref), (tdir_hbm, tdir_ref), (base_hbm, base_ref), (inj_hbm, inj_ref)))
    ]
    for load in loads[:5]:
        load.start()
    rock = lax.axis_index("rock")
    plane = lax.axis_index("plane")
    here = rock * TILES + plane
    nxt = lax.rem(here + 1, PARTS)
    prv = lax.rem(here + PARTS - 1, PARTS)
    next_part = (lax.div(nxt, TILES), lax.rem(nxt, TILES))
    prev_part = (lax.div(prv, TILES), lax.rem(prv, TILES))
    next_tile = (rock, lax.rem(plane + 1, TILES))
    prev_tile = (rock, lax.rem(plane + TILES - 1, TILES))

    def peer(o):
        return lax.rem(plane + o, TILES)

    barrier = pltpu.get_barrier_semaphore()
    for target in (next_part, prev_part):
        pl.semaphore_signal(barrier, inc=1, device_id=target, device_id_type=MESH)

    def greet(o, carry):
        pl.semaphore_signal(barrier, inc=1, device_id=(rock, peer(o)), device_id_type=MESH)
        return carry

    lax.fori_loop(1, TILES, greet, 0)
    for load in loads[5:]:
        load.start()

    def pair(outs, ins, index):
        return [
            pltpu.make_async_remote_copy(
                outs.at[0], ins.at[1], halo_send.at[index], halo_recv.at[index],
                device_id=prev_part, device_id_type=MESH),
            pltpu.make_async_remote_copy(
                outs.at[1], ins.at[0], halo_send.at[index + 1], halo_recv.at[index + 1],
                device_id=next_part, device_id_type=MESH),
        ]

    def edges(index):
        return [
            pltpu.make_async_remote_copy(
                edge_out.at[2 * index], edge_in.at[2 * index + 1], edge_send.at[2 * index],
                edge_recv.at[2 * index], device_id=prev_tile, device_id_type=MESH),
            pltpu.make_async_remote_copy(
                edge_out.at[2 * index + 1], edge_in.at[2 * index], edge_send.at[2 * index + 1],
                edge_recv.at[2 * index + 1], device_id=next_tile, device_id_type=MESH),
        ]

    def swap(outs, ins, sends, recvs, o):
        return pltpu.make_async_remote_copy(
            outs.at[peer(o)], ins.at[plane], sends.at[o - 1], recvs.at[o - 1],
            device_id=(rock, peer(o)), device_id_type=MESH)

    def start_all(*what):
        def one(o, carry):
            swap(*what, o).start()
            return carry
        lax.fori_loop(1, TILES, one, 0)
        outs, ins = what[:2]
        ins[plane] = outs[plane]

    def arrive_all(*what):
        def one(o, carry):
            swap(*what, o).wait_recv()
            return carry
        lax.fori_loop(1, TILES, one, 0)

    def sent_all(*what):
        def one(o, carry):
            swap(*what, o).wait_send()
            return carry
        lax.fori_loop(1, TILES, one, 0)

    for load in loads[:5]:
        load.wait()
    tmap = tmap_ref[...]
    lift = lift_ref[...]
    widen = ones_where(iota((Q, QB), 0) == iota((Q, QB), 1)).astype(BF16)
    th, tl = split(padded(tmap, QB))
    tw[0:QB, :] = dot(th, widen).astype(BF16)
    tw[QB:2 * QB, :] = dot(tl, widen).astype(BF16)

    same = ones_where(lax.rem(iota((Q, Q), 0), 9) == lax.rem(iota((Q, Q), 1), 9))
    odir = odir_ref[...]
    of_face = jnp.where(lax.div(iota((16, Q), 0), 4) == lax.div(iota((16, Q), 1), 9), exact_dot(odir, lift), 0.0)
    of_face = exact_dot(of_face, same)
    gh, gl = split(jnp.where(lax.rem(iota((16, Q), 0), 4) == lax.div(iota((16, Q), 1), 9), of_face, 0.0))
    gw[0:16, :] = dot(gh, widen).astype(BF16)
    gw[16:32, :] = dot(gl, widen).astype(BF16)

    def scores_of(x):
        high, rest = split(padded(x, QB))
        got = dot(gw[...], high)
        return got[0:16] + got[16:32] + dot(gw[0:16, :], rest)

    def put_scores(got, start):
        for l in range(got.shape[1] // 256):
            for half in range(2):
                at = 256 * l + 128 * half
                gtab[half, pl.ds(start + l, 16, stride=16), :] = got[:, at:at + 128]

    def put_state(x):
        high, rest = split(padded(x, QB))
        xh[0:QB, :] = high
        xl[0:QB, :] = rest

    def traces():
        first = dot(tw[...], xh[0:QB, :])
        return first[0:QP] + first[QB:QB + QP] + dot(tw[0:QB, :], xl[0:QB, :])[0:QP]

    def put_table(parts, start):
        rows = jnp.concatenate(
            [x[:, 256 * l:256 * l + 256] for x in parts for l in range(x.shape[1] // 256)], axis=0)
        high, rest = split(rows)
        table[start:start + rows.shape[0], 0:256] = high
        table[start:start + rows.shape[0], 256:512] = rest

    def pick(got, rows, which, first, count):
        for l in range(count):
            part = rows[QP * l:QP * l + QP]
            got = part if got is None else jnp.where(which == first + l, part, got)
        return got

    def fill_outgoing(out):
        for side in range(2):
            a = send_hot[:, HALO * side:HALO * side + HALO]
            rows = dot(table[0:320, :], jnp.concatenate([a, a], axis=0))
            out[side] = pick(None, rows, send_ref[side:side + 1, :] >> 8, 0, 8)

    def rims(rim):
        lower = jnp.where(here > 0, rim[0], 0.0)
        upper = jnp.where(here < PARTS - 1, rim[1], 0.0)
        return lower, upper

    face_of_row = lax.div(iota((QP, 1), 0), 9)

    def columns(k, rows):
        a = hot[:, ELEMS * k:ELEMS * k + ELEMS]
        return dot(rows, jnp.concatenate([a, a], axis=0))

    def put_faces(k, got):
        got = jnp.where(face_of_row == nfa_ref[k:k + 1, :], got, 0.0)
        high, rest = split(padded(got, QB))
        xh[QB * (k + 1):QB * (k + 2), :] = high
        xl[QB * (k + 1):QB * (k + 2), :] = rest

    def gather_faces(k):
        put_faces(k, pick(None, columns(k, table[...]), nel_ref[k:k + 1, :] >> 8, 0, 16))

    def gather_own(k):
        own2[k] = pick(None, columns(k, table[0:320, :]), nel_ref[k:k + 1, :] >> 8, 0, 8)

    def gather_rims(k):
        put_faces(k, pick(own2[k], columns(k, table[320:640, :]), nel_ref[k:k + 1, :] >> 8, 8, 8))

    def change():
        first = dot(ww[...], xh[...])
        return first[0:QP] + first[QB:QB + QP] + dot(ww[0:QB, :], xl[...])[0:QP]

    s1[0:Q, :] = state_ref[...]
    s1[Q:QP, :] = jnp.zeros((QP - Q, ELEMS), F32)
    put_state(s1[...])
    tr = traces()
    put_table([tr], 0)

    for side in range(2):
        send_hot[:, HALO * side:HALO * side + HALO] = units(256, send_ref[side:side + 1, :] & 255)
    fill_outgoing(out1)
    for side in range(2):
        gout[side] = scores_of(out1[side])
    pl.semaphore_wait(barrier, TILES + 1)
    for copy in pair(gout, grim, 6) + pair(out1, rim1, 0):
        copy.start()
    for load in loads[5:]:
        load.wait()
    edge_out[0] = press_ref[pl.ds(0, 64, stride=2), :]
    edge_out[1] = press_ref[pl.ds(1, 64, stride=2), :]
    for copy in edges(0):
        copy.start()

    tile = ftile_ref[...]
    upper = ones_where(iota((128, 128), 0) <= iota((128, 128), 1)).astype(BF16)
    count = jnp.concatenate([upper, jnp.ones((128, 128), BF16)], axis=0)
    before = ones_where(iota((64, 64), 1) < iota((64, 64), 0)).astype(BF16)
    named = [ones_where(tile == t).astype(BF16) for t in range(TILES)]
    earlier = dot(before, jnp.concatenate(named, axis=1)).astype(BF16)
    ranks = dot(
        jnp.concatenate(
            [jnp.concatenate([named[t], earlier[:, 128 * t:128 * t + 128]], axis=1) for t in range(TILES)],
            axis=0),
        count)
    place = jnp.zeros((64, 128), F32)
    for t in range(TILES):
        place = jnp.where(tile == t, ranks[64 * t:64 * t + 64] + (512.0 * t - 1.0), place)
    place = place.astype(I32)
    cell = fcell_ref[...]
    elem = fel_ref[...]
    row = ((cell >> 7) & 63) * 2 + (cell >> 13)
    code = (row & 63) * 256 + (row >> 6) * 128 + (cell & 127)
    slot = iota((64, 128), 0) * 128 + iota((64, 128), 1)
    live = jnp.where(slot < fcount_ref[0], 128, 0)
    slot_tab[0] = (place >> 7).astype(F32)
    slot_tab[1] = (place & 127).astype(F32)
    slot_tab[2] = ((code >> 5) - 256).astype(F32)
    slot_tab[3] = ((code & 31) * 16 + (elem >> 7) - 256).astype(F32)
    slot_tab[4] = ((elem & 127) + live).astype(F32)

    row64 = iota((64, 128), 0).astype(F32)
    row128 = iota((128, 128), 0).astype(F32)

    def order_body(half, total):
        named = []
        inner = []
        for u in range(32):
            at = pl.ds(32 * half + u, 1)
            mine = row64 == slot_tab[0, at, :]
            named.append(jnp.concatenate(
                [jnp.where(mine, slot_tab[2 + v, at, :], 0.0).astype(BF16) for v in range(3)], axis=0))
            inner.append(ones_where(row128 == slot_tab[1, at, :]).astype(BF16))
        return total + dot_nt(jnp.concatenate(named, axis=1), jnp.concatenate(inner, axis=1))

    grouped = lax.fori_loop(0, 2, order_body, jnp.zeros((192, 128), F32)).astype(I32)
    middle = grouped[64:128] + 256
    code = ((grouped[0:64] + 256) * 32 + (middle >> 4)).astype(F32)
    high = ((middle & 15) + ((grouped[128:192] >> 7) << 4)).astype(F32)
    low = (grouped[128:192] & 127).astype(F32)
    for c in range(64):
        at = slice(128 * c, 128 * c + 128)
        inner = slice(128 * (c % 4), 128 * (c % 4) + 128)
        cells_out[c // 4, :, inner] = code[c:c + 1]
        elem_hi[:, at] = high[c:c + 1]
        elem_lo[:, at] = low[c:c + 1]
    start_all(cells_out, cells_in, cell_send, cell_recv)

    for k in range(4):
        hot[:, ELEMS * k:ELEMS * k + ELEMS] = units(256, nel_ref[k:k + 1, :] & 255)

    for k in range(4):
        at = slice(2048 * k, 2048 * k + 2048)
        elem_hot[:, at] = units(128, elem_lo[:, at].astype(I32))

    volume = stiff_ref[...] - exact_dot(lift, tmap)
    put_scores(scores_of(tr), 0)
    scale = STEP * jac_ref[...]
    own_state = s1[...]
    direct = jnp.sum(column(odir) * own_state, axis=0, keepdims=True)
    within = jnp.sum(column(exact_dot(odir, volume)) * own_state, axis=0, keepdims=True)

    for copy in pair(gout, grim, 6):
        copy.wait_recv()
    for side, got in enumerate(rims(grim)):
        put_scores(got, 8 + 4 * side)
    for k in range(4):
        at = slice(64 * k, 64 * k + 64)
        gh, gl = split(jnp.concatenate([gtab[0, at, :], gtab[1, at, :]], axis=1))
        got = dot(jnp.concatenate([gh, gl], axis=0), hot[:, ELEMS * k:ELEMS * k + ELEMS])
        mine = iota((64, ELEMS), 0) == nfa_ref[k:k + 1, :] * 16 + (nel_ref[k:k + 1, :] >> 8)
        within = within + jnp.sum(jnp.where(mine, got[0:64] + got[64:128], 0.0), axis=0, keepdims=True)
    score = direct + scale * within

    opening = 0.2 * (jnp.maximum(score, 0.0) + jnp.log1p(jnp.exp(-jnp.abs(score))))
    oh, ol = split(jnp.concatenate([opening[:, 128 * i:128 * i + 128] for i in range(16)], axis=0))
    got = dot(jnp.concatenate([oh, ol], axis=0), elem_hot[...])
    sixteen = (iota((16, 1), 0) + 16).astype(F32)
    picked = jnp.sum(
        jnp.where(sixteen == elem_hi[...], got[0:16] + got[16:32], 0.0), axis=0, keepdims=True)
    for t in range(TILES):
        open_out[t] = picked[:, 512 * t:512 * t + 512]
    start_all(open_out, open_in, open_send, open_recv)

    arrive_all(cells_out, cells_in, cell_send, cell_recv)

    for t in range(TILES):
        at = slice(512 * t, 512 * t + 512)
        where = cells_in[t].astype(I32)
        cell_hot[:, at] = units(256, where & 255)
        cell_unit[:, at] = units(64, where >> 8)
        cell_row[:, at] = where >> 8

    row_i = iota((Q, 256), 0)
    col_i = iota((Q, 256), 1)
    own_block = ones_where(row_i == col_i).astype(BF16)
    blk = lax.div(col_i, QB)
    inner = lax.rem(col_i, QB)
    face_block = ones_where(
        (blk >= 1) & (blk <= 4) & (inner < Q) & (row_i == 9 * (blk - 1) + lax.rem(inner, 9))).astype(BF16)
    mh, ml = split(padded(volume, QB))
    lh, ll = split(padded(lift, QB))
    ww[0:QB, :] = (dot(mh, own_block) + dot(lh, face_block)).astype(BF16)
    ww[QB:2 * QB, :] = (dot(ml, own_block) + dot(ll, face_block)).astype(BF16)
    xh[5 * QB:256, :] = jnp.zeros((16, ELEMS), BF16)
    xl[5 * QB:256, :] = jnp.zeros((16, ELEMS), BF16)
    for copy in pair(out1, rim1, 0):
        copy.wait_recv()
    put_table(list(rims(rim1)), 320)
    gather_faces(0)
    gather_faces(1)

    arrive_all(open_out, open_in, open_send, open_recv)

    amounts = []
    for t in range(TILES):
        high = open_in[t].astype(BF16).astype(F32)
        unit = cell_unit[:, 512 * t:512 * t + 512]
        amounts.append(jnp.concatenate(
            [unit * jnp.concatenate([jnp.broadcast_to(part, (16, 512)).astype(BF16)] * 4, axis=0)
             for part in (high, open_in[t] - high)], axis=0))
    field = dot_nt(jnp.concatenate(amounts, axis=1), cell_hot[...])
    field = field[0:64] + field[64:128]
    aper = base_ref[...] + jnp.concatenate([field[:, 0:128], field[:, 128:256]], axis=0)
    aper_ref[...] = aper
    c = aper * aper * aper / 12.0
    cond[...] = c
    edge_out[2] = cond[pl.ds(0, 64, stride=2), :]
    edge_out[3] = cond[pl.ds(1, 64, stride=2), :]
    for copy in edges(1):
        copy.start()

    gather_faces(2)
    gather_faces(3)
    s1[...] = s1[...] + scale * change()

    put_state(s1[...])
    put_table([traces()], 0)
    fill_outgoing(out2)
    for copy in pair(out2, rim2, 2):
        copy.start()
    p = press_ref[...]
    odd = (iota((128, 128), 0) & 1) == 1
    lane = iota((128, 128), 1)
    block = iota((128, 128), 0) >> 1
    for copy in edges(0) + edges(1):
        copy.wait_recv()
    for i in range(2):
        edge_wide[i, pl.ds(0, 64, stride=2), :] = edge_in[2 * i]
        edge_wide[i, pl.ds(1, 64, stride=2), :] = edge_in[2 * i + 1]

    def sides(x, wide):
        after = pltpu.roll(x, 127, 1)
        after = jnp.where(lane == 127, pltpu.roll(after, 126, 0), after)
        ahead = pltpu.roll(x, 1, 1)
        ahead = jnp.where(lane == 0, pltpu.roll(ahead, 2, 0), ahead)
        up = jnp.where(odd, pltpu.roll(x, 1, 0), wide)
        down = jnp.where(odd, wide, pltpu.roll(x, 127, 0))
        inside = (
            (lane < 127) | (block < 63),
            (lane > 0) | (block > 0),
            odd | (plane > 0),
            jnp.logical_not(odd) | (plane < TILES - 1),
        )
        return [jnp.where(m, v, 0.0) for m, v in zip(inside, (after, ahead, up, down))]

    inflow = jnp.zeros((128, 128), F32)
    for other_p, other_c in zip(sides(p, edge_wide[0]), sides(c, edge_wide[1])):
        inflow = inflow + 2.0 * c * other_c / (c + other_c) * (other_p - p)
    new_p = p + RATE * (inflow + inj_ref[...])
    new_press_ref[...] = new_p

    ph, prest = split(jnp.concatenate([new_p[0:64], new_p[64:128]], axis=1))
    pressures = jnp.concatenate([ph, prest], axis=0)
    for b in range(4):
        at = slice(2048 * b, 2048 * b + 2048)
        got = dot(pressures, cell_hot[:, at])
        mine = iota((64, 2048), 0) == cell_row[:, at]
        picked = jnp.sum(jnp.where(mine, got[0:64] + got[64:128], 0.0), axis=0, keepdims=True)
        for t in range(4):
            press_out[4 * b + t] = picked[:, 512 * t:512 * t + 512]
    start_all(press_out, press_in, pr_send, pr_recv)

    for k in range(4):
        gather_own(k)

    push = column(tdir_ref[...])
    tau = exact_dot(tmap, push[0:Q])
    of_facet = jnp.where(lax.div(iota((Q, 128), 0), 9) == lax.rem(iota((Q, 128), 1), 4), tau, 0.0)
    spread = jnp.where(
        lax.div(iota((Q, 128), 0), 9) == lax.div(iota((Q, 128), 1), 4), exact_dot(same, of_facet), 0.0)
    load_map = jnp.where(
        iota((Q, 128), 1) == 16, exact_dot(volume, push[0:Q]), exact_dot(lift, spread))
    uh, ul = split(padded(load_map, QB))
    uu[0:QB, :] = uh
    uu[QB:2 * QB, :] = ul
    arrive_all(press_out, press_in, pr_send, pr_recv)

    for t in range(TILES):
        slot_row[:, 512 * t:512 * t + 512] = press_in[t]
    high, rest = split(jnp.where(sixteen == elem_hi[...], slot_row[...], 0.0))
    load = dot_nt(jnp.concatenate([high, rest], axis=0), elem_hot[...])
    load = load[0:16] + load[16:32]
    for i in range(16):
        lane_row[:, 128 * i:128 * i + 128] = load[i:i + 1]
    w = scale * lane_row[...]
    own_w = jnp.concatenate([w[:, 256 * l:256 * l + 256] for l in range(8)], axis=0)
    wh, wl = split(own_w)
    got = dot(jnp.concatenate([wh, wl], axis=0), send_hot[...])
    got = got[0:8] + got[8:16]
    for side in range(2):
        mine = iota((8, HALO), 0) == (send_ref[side:side + 1, :] >> 8)
        wout[side] = jnp.sum(
            jnp.where(mine, got[:, HALO * side:HALO * side + HALO], 0.0), axis=0, keepdims=True)
    for copy in pair(wout, wrim, 4):
        copy.start()
    for copy in pair(out2, rim2, 2):
        copy.wait_recv()
    put_table(list(rims(rim2)), 320)
    for k in range(4):
        gather_rims(k)
    change2 = change()
    for copy in pair(wout, wrim, 4):
        copy.wait_recv()
    low, high_rim = rims(wrim)
    far_w = jnp.concatenate([x[:, 256 * l:256 * l + 256] for x in (low, high_rim) for l in range(4)], axis=0)
    wh, wl = split(jnp.concatenate([own_w, far_w], axis=0))
    got = dot(jnp.concatenate([wh, wl], axis=0), hot[...])
    got = got[0:16] + got[16:32]
    near = []
    for k in range(4):
        mine = iota((16, ELEMS), 0) == (nel_ref[k:k + 1, :] >> 8)
        near_w = jnp.sum(jnp.where(mine, got[:, ELEMS * k:ELEMS * k + ELEMS], 0.0), axis=0, keepdims=True)
        near.append(jnp.where(iota((4, ELEMS), 0) == nfa_ref[k:k + 1, :], near_w, 0.0))
    near.append(w)
    near.append(jnp.zeros((128 - 17, ELEMS), F32))
    nh, nl = split(jnp.concatenate(near, axis=0))
    first = dot(uu[...], nh)
    extra = first[0:QP] + first[QB:QB + QP] + dot(uu[0:QB, :], nl)[0:QP]
    result = s1[...] + push * w + scale * (change2 + extra)
    new_state_ref[...] = result[0:Q]

    for index, (outs, ins) in enumerate(((out1, rim1), (out2, rim2), (wout, wrim), (gout, grim))):
        for copy in pair(outs, ins, 2 * index):
            copy.wait_send()
    for copy in edges(0) + edges(1):
        copy.wait_send()
    sent_all(cells_out, cells_in, cell_send, cell_recv)
    sent_all(open_out, open_in, open_send, open_recv)
    sent_all(press_out, press_in, pr_send, pr_recv)


def hand_over(*refs):
    sources, targets, held, sems = refs[0:3], refs[3:6], refs[6:9], refs[9]
    arrive = [pltpu.make_async_copy(sources[i], held[i], sems.at[i]) for i in range(3)]
    leave = [pltpu.make_async_copy(held[i], targets[i], sems.at[3 + i]) for i in range(3)]
    for copy in arrive:
        copy.start()
    for first, then in zip(arrive, leave):
        first.wait()
        then.start()
    for copy in leave:
        copy.wait()


def interleaved(x):
    return x.reshape(2, 64, 128).transpose(1, 0, 2).reshape(128, 128)


def straight(x):
    return x.reshape(64, 2, 128).transpose(1, 0, 2).reshape(1, 2, 8192)


def shards(
    rock_state, jacobian, stiffness, trace_map, lift_map, neighbor_elem, neighbor_face, send_elem,
    opening_dir, traction_dir, face_elem, face_tile, face_cell, face_count, pressure, base_aperture, injection,
):
    vmem = pl.BlockSpec(memory_space=pltpu.VMEM)
    hbm = pl.BlockSpec(memory_space=pltpu.HBM)
    smem = pl.BlockSpec(memory_space=pltpu.SMEM)
    scratch = [
        pltpu.VMEM((QP, ELEMS), F32),
        pltpu.VMEM((640, 512), BF16),
        pltpu.VMEM((256, SLOTS), BF16),
        pltpu.VMEM((256, 2 * HALO), BF16),
        pltpu.VMEM((256, ELEMS), BF16),
        pltpu.VMEM((256, ELEMS), BF16),
        pltpu.VMEM((2 * QB, 256), BF16),
        pltpu.VMEM((2 * QB, QB), BF16),
        pltpu.VMEM((2 * QB, 128), BF16),
        pltpu.VMEM((32, QB), BF16),
        pltpu.VMEM((2, 256, 128), F32),
        pltpu.VMEM((2, QP, HALO), F32),
        pltpu.VMEM((2, QP, HALO), F32),
        pltpu.VMEM((2, QP, HALO), F32),
        pltpu.VMEM((2, QP, HALO), F32),
        pltpu.VMEM((2, 1, HALO), F32),
        pltpu.VMEM((2, 1, HALO), F32),
        pltpu.VMEM((2, 16, HALO), F32),
        pltpu.VMEM((2, 16, HALO), F32),
        pltpu.VMEM((128, SLOTS), BF16),
        pltpu.VMEM((1, SLOTS), F32),
        pltpu.VMEM((1, SLOTS), F32),
        pltpu.VMEM((TILES, 1, 512), F32),
        pltpu.VMEM((TILES, 1, 512), F32),
        pltpu.VMEM((TILES, 1, 512), F32),
        pltpu.VMEM((TILES, 1, 512), F32),
        pltpu.VMEM((TILES, 1, 512), F32),
        pltpu.VMEM((TILES, 1, 512), F32),
        pltpu.VMEM((5, 64, 128), F32),
        pltpu.VMEM((256, SLOTS), BF16),
        pltpu.VMEM((64, SLOTS), BF16),
        pltpu.VMEM((1, SLOTS), I32),
        pltpu.VMEM((128, 128), F32),
        pltpu.VMEM((4, 64, 128), F32),
        pltpu.VMEM((4, 64, 128), F32),
        pltpu.VMEM((2, 128, 128), F32),
        pltpu.VMEM((4, QP, ELEMS), F32),
        pltpu.VMEM((1, ELEMS), F32),
        pltpu.VMEM((1, SLOTS), F32),
        pltpu.VMEM((Q, ELEMS), F32),
        pltpu.VMEM((1, ELEMS), F32),
        pltpu.VMEM((Q, Q), F32),
        pltpu.VMEM((Q, Q), F32),
        pltpu.VMEM((Q, Q), F32),
        pltpu.VMEM((4, ELEMS), I32),
        pltpu.VMEM((4, ELEMS), I32),
        pltpu.VMEM((2, HALO), I32),
        pltpu.VMEM((1, Q), F32),
        pltpu.VMEM((1, Q), F32),
        pltpu.VMEM((64, 128), I32),
        pltpu.VMEM((64, 128), I32),
        pltpu.VMEM((64, 128), I32),
        pltpu.VMEM((128, 128), F32),
        pltpu.VMEM((128, 128), F32),
        pltpu.VMEM((128, 128), F32),
    ] + [pltpu.SemaphoreType.DMA((n,)) for n in (16, 8, 8, 15, 15, 15, 15, 15, 15, 4, 4)]
    new_state, new_pressure, aperture = pl.pallas_call(
        kernel,
        out_shape=(
            jax.ShapeDtypeStruct((Q, ELEMS), F32),
            jax.ShapeDtypeStruct((128, 128), F32),
            jax.ShapeDtypeStruct((128, 128), F32),
        ),
        in_specs=[hbm] * 13 + [smem] + [hbm] * 3,
        out_specs=(vmem,) * 3,
        scratch_shapes=scratch,
        compiler_params=pltpu.CompilerParams(
            collective_id=0, has_side_effects=True, vmem_limit_bytes=56 * 2**20),
    )(
        rock_state, jacobian.reshape(1, ELEMS), stiffness, trace_map, lift_map, neighbor_elem, neighbor_face,
        send_elem, opening_dir.reshape(1, Q), traction_dir.reshape(1, Q), face_elem.reshape(64, 128),
        face_tile.reshape(64, 128), face_cell.reshape(64, 128), face_count, interleaved(pressure),
        interleaved(base_aperture), interleaved(injection),
    )
    results = (new_state, new_pressure, aperture)
    new_state, new_pressure, aperture = pl.pallas_call(
        hand_over,
        out_shape=tuple(jax.ShapeDtypeStruct(x.shape, F32) for x in results),
        in_specs=[hbm] * 3,
        out_specs=(hbm,) * 3,
        scratch_shapes=[pltpu.VMEM(x.shape, F32) for x in results] + [pltpu.SemaphoreType.DMA((6,))],
    )(*results)
    return new_state, straight(new_pressure), straight(aperture)


def solution(mesh):
    elems = P(None, ("rock", "plane"))
    flat = P(("rock", "plane"))
    grid = P("rock", "plane", None)
    return jax.shard_map(
        shards,
        mesh=mesh,
        in_specs=(elems, flat, P(), P(), P(), elems, elems, elems, P(), P(), flat, flat, flat, flat, grid, grid, grid),
        out_specs=(elems, grid, grid),
        check_vma=False,
    )
```

```python
import jax
import jax.numpy as jnp
from jax import lax
from jax.experimental import pallas as pl
from jax.experimental.pallas import tpu as pltpu
from jax.sharding import PartitionSpec as P

STEP = 0.25
RATE = 0.35
F32 = jnp.float32
BF16 = jnp.bfloat16
I32 = jnp.int32
MESH = pl.DeviceIdType.MESH
Q = 36
QP = 40
QB = 48
ELEMS = 2048
HALO = 1024
SLOTS = 8192
TILES = 16
PARTS = 128
FAR = [(a, b) for a in (1, 2, 3) for b in (1, 2, 3)]
NEAR = [(0, 1), (0, 2), (0, 3), (1, 0), (2, 0), (3, 0)]
STEPS = FAR + NEAR


def dot(a, b):
    return jnp.dot(a, b, preferred_element_type=F32)


def dot_nt(a, b):
    return lax.dot_general(a, b, (((1,), (1,)), ((), ())), preferred_element_type=F32)


def exact_dot(a, b):
    return jnp.dot(a, b, preferred_element_type=F32, precision=lax.Precision.HIGHEST)


def split(x):
    high = x.astype(BF16)
    return high, (x - high.astype(F32)).astype(BF16)


def iota(shape, dim):
    return lax.broadcasted_iota(I32, shape, dim)


def ones_where(mask):
    return jnp.where(mask, 1.0, 0.0).astype(F32)


def units(count, row):
    return ones_where(iota((count, row.shape[1]), 0) == row).astype(BF16)


def lanes(chunk, width=128):
    return pl.ds(pl.multiple_of(chunk * width, width), width)


def padded(x, rows):
    return jnp.concatenate([x, jnp.zeros((rows - x.shape[0],) + x.shape[1:], x.dtype)], axis=0)


def column(row):
    wide = jnp.broadcast_to(row, (QP, Q))
    eye = iota((QP, Q), 0) == iota((QP, Q), 1)
    return jnp.sum(jnp.where(eye, wide, 0.0), axis=1, keepdims=True)


def kernel(
    state_hbm, jac_hbm, stiff_hbm, tmap_hbm, lift_hbm, nel_hbm, nfa_hbm, send_hbm, odir_hbm, tdir_hbm,
    fel_hbm, ftile_hbm, fcell_hbm, fcount_ref, press_hbm, base_hbm, inj_hbm,
    new_state_ref, new_press_ref, aper_ref,
    s1, table, hot, send_hot, xh, xl, ww, tw, uu, gw, gtab, out1, out2, rim1, rim2, wout, wrim, gout, grim,
    elem_hot, elem_hi, elem_lo, cells_out, cells_in, open_out, open_in, press_out, press_in,
    slot_tab, cell_hot, cell_unit, cell_row, cond, edge_out, edge_in, edge_wide, own2, lane_row,
    state_ref, jac_ref, stiff_ref, tmap_ref, lift_ref, nel_ref, nfa_ref, send_ref, odir_ref, tdir_ref,
    fel_ref, ftile_ref, fcell_ref, press_ref, base_ref, inj_ref, in_sem,
    halo_send, halo_recv, cell_send, cell_recv, open_send, open_recv, pr_send, pr_recv, edge_send, edge_recv,
):
    loads = [
        pltpu.make_async_copy(source, target, in_sem.at[i])
        for i, (source, target) in enumerate((
            (state_hbm, state_ref), (tmap_hbm, tmap_ref), (send_hbm, send_ref), (lift_hbm, lift_ref),
            (odir_hbm, odir_ref), (ftile_hbm, ftile_ref), (fcell_hbm, fcell_ref), (fel_hbm, fel_ref), (press_hbm, press_ref),
            (nel_hbm, nel_ref), (nfa_hbm, nfa_ref), (stiff_hbm, stiff_ref),
            (jac_hbm, jac_ref), (tdir_hbm, tdir_ref), (base_hbm, base_ref), (inj_hbm, inj_ref)))
    ]
    loads[0].start()
    rock = lax.axis_index("rock")
    plane = lax.axis_index("plane")
    here = rock * TILES + plane
    nxt = lax.rem(here + 1, PARTS)
    prv = lax.rem(here + PARTS - 1, PARTS)
    next_part = (lax.div(nxt, TILES), lax.rem(nxt, TILES))
    prev_part = (lax.div(prv, TILES), lax.rem(prv, TILES))
    next_tile = (rock, lax.rem(plane + 1, TILES))
    prev_tile = (rock, lax.rem(plane + TILES - 1, TILES))

    def tile_at(a, b):
        return lax.rem(lax.div(plane, 4) + a, 4) * 4 + lax.rem(lax.rem(plane, 4) + b, 4)

    targets = [tile_at(a, b) for a, b in STEPS]
    sources = [tile_at(4 - a, 4 - b) for a, b in STEPS]
    far_tiles = sources[:len(FAR)]
    near_tiles = [plane] + sources[len(FAR):]

    barrier = pltpu.get_barrier_semaphore()
    for target in (next_part, prev_part):
        pl.semaphore_signal(barrier, inc=1, device_id=target, device_id_type=MESH)

    for target in targets:
        pl.semaphore_signal(barrier, inc=1, device_id=(rock, target), device_id_type=MESH)
    for load in loads[1:]:
        load.start()

    def pair(outs, ins, index):
        return [
            pltpu.make_async_remote_copy(
                outs.at[0], ins.at[1], halo_send.at[index], halo_recv.at[index],
                device_id=prev_part, device_id_type=MESH),
            pltpu.make_async_remote_copy(
                outs.at[1], ins.at[0], halo_send.at[index + 1], halo_recv.at[index + 1],
                device_id=next_part, device_id_type=MESH),
        ]

    def edges(index):
        return [
            pltpu.make_async_remote_copy(
                edge_out.at[2 * index], edge_in.at[2 * index + 1], edge_send.at[2 * index],
                edge_recv.at[2 * index], device_id=prev_tile, device_id_type=MESH),
            pltpu.make_async_remote_copy(
                edge_out.at[2 * index + 1], edge_in.at[2 * index], edge_send.at[2 * index + 1],
                edge_recv.at[2 * index + 1], device_id=next_tile, device_id_type=MESH),
        ]

    def swap(outs, ins, sends, recvs, o):
        return pltpu.make_async_remote_copy(
            outs.at[targets[o]], ins.at[plane], sends.at[o], recvs.at[o],
            device_id=(rock, targets[o]), device_id_type=MESH)

    def start_all(*what):
        for o in range(len(STEPS)):
            swap(*what, o).start()
        outs, ins = what[:2]
        ins[plane] = outs[plane]

    def arrive_far(*what):
        for o in range(len(FAR)):
            swap(*what, o).wait_recv()

    def arrive_near(*what):
        for o in range(len(FAR), len(STEPS)):
            swap(*what, o).wait_recv()

    def sent_all(*what):
        for o in range(len(STEPS)):
            swap(*what, o).wait_send()

    for load in loads[:5]:
        load.wait()
    tmap = tmap_ref[...]
    lift = lift_ref[...]
    widen = ones_where(iota((Q, QB), 0) == iota((Q, QB), 1)).astype(BF16)
    th, tl = split(padded(tmap, QB))
    tw[0:QB, :] = dot(th, widen).astype(BF16)
    tw[QB:2 * QB, :] = dot(tl, widen).astype(BF16)

    same = ones_where(lax.rem(iota((Q, Q), 0), 9) == lax.rem(iota((Q, Q), 1), 9))
    odir = odir_ref[...]
    of_face = jnp.where(lax.div(iota((16, Q), 0), 4) == lax.div(iota((16, Q), 1), 9), exact_dot(odir, lift), 0.0)
    of_face = exact_dot(of_face, same)
    gh, gl = split(jnp.where(lax.rem(iota((16, Q), 0), 4) == lax.div(iota((16, Q), 1), 9), of_face, 0.0))
    gw[0:16, :] = dot(gh, widen).astype(BF16)
    gw[16:32, :] = dot(gl, widen).astype(BF16)

    def scores_of(x):
        high, rest = split(padded(x, QB))
        got = dot(gw[...], high)
        return got[0:16] + got[16:32] + dot(gw[0:16, :], rest)

    def put_scores(got, start):
        for l in range(got.shape[1] // 256):
            for half in range(2):
                at = 256 * l + 128 * half
                gtab[half, pl.ds(start + l, 16, stride=16), :] = got[:, at:at + 128]

    def put_state(x):
        high, rest = split(padded(x, QB))
        xh[0:QB, :] = high
        xl[0:QB, :] = rest

    def traces():
        first = dot(tw[...], xh[0:QB, :])
        return first[0:QP] + first[QB:QB + QP] + dot(tw[0:QB, :], xl[0:QB, :])[0:QP]

    def put_table(parts, start):
        rows = jnp.concatenate(
            [x[0:Q, 256 * l:256 * l + 256] for x in parts for l in range(x.shape[1] // 256)], axis=0)
        high, rest = split(rows)
        table[start:start + rows.shape[0], 0:256] = high
        table[start:start + rows.shape[0], 256:512] = rest

    def pick(got, rows, which, first, count):
        for l in range(count // 2):
            part = rows[2 * Q * l:2 * Q * l + 2 * Q]
            got = part if got is None else jnp.where((which >> 1) == first // 2 + l, part, got)
        return got

    def one_of(got, which):
        return jnp.where((which & 1) == 1, got[Q:2 * Q], got[0:Q])

    def fill_outgoing(out):
        for side in range(2):
            a = send_hot[:, HALO * side:HALO * side + HALO]
            which = send_ref[side:side + 1, :] >> 8
            rows = dot(table[0:8 * Q, :], jnp.concatenate([a, a], axis=0))
            out[side] = padded(one_of(pick(None, rows, which, 0, 8), which), QP)

    def rims(rim):
        lower = jnp.where(here > 0, rim[0], 0.0)
        upper = jnp.where(here < PARTS - 1, rim[1], 0.0)
        return lower, upper

    face_of_row = lax.div(iota((Q, 1), 0), 9)

    def columns(k, rows):
        a = hot[:, ELEMS * k:ELEMS * k + ELEMS]
        return dot(rows, jnp.concatenate([a, a], axis=0))

    def put_faces(k, got):
        got = jnp.where(face_of_row == nfa_ref[k:k + 1, :], got, 0.0)
        high, rest = split(padded(got, QB))
        xh[QB * (k + 1):QB * (k + 2), :] = high
        xl[QB * (k + 1):QB * (k + 2), :] = rest

    def gather_faces(k):
        which = nel_ref[k:k + 1, :] >> 8
        put_faces(k, one_of(pick(None, columns(k, table[...]), which, 0, 16), which))

    def gather_own(k):
        own2[k] = pick(None, columns(k, table[0:8 * Q, :]), nel_ref[k:k + 1, :] >> 8, 0, 8)

    def gather_rims(k):
        which = nel_ref[k:k + 1, :] >> 8
        put_faces(k, one_of(pick(own2[k], columns(k, table[8 * Q:, :]), which, 8, 8), which))

    def change():
        first = dot(ww[...], xh[...])
        return first[0:QP] + first[QB:QB + QP] + dot(ww[0:QB, :], xl[...])[0:QP]

    s1[0:Q, :] = state_ref[...]
    s1[Q:QP, :] = jnp.zeros((QP - Q, ELEMS), F32)
    put_state(s1[...])
    tr = traces()
    put_table([tr], 0)

    for side in range(2):
        send_hot[:, HALO * side:HALO * side + HALO] = units(256, send_ref[side:side + 1, :] & 255)
    fill_outgoing(out1)
    for side in range(2):
        gout[side] = scores_of(out1[side])
    pl.semaphore_wait(barrier, TILES + 1)
    for copy in pair(gout, grim, 6) + pair(out1, rim1, 0):
        copy.start()
    for load in loads[5:]:
        load.wait()
    edge_out[0] = press_ref[pl.ds(0, 64, stride=2), :]
    edge_out[1] = press_ref[pl.ds(1, 64, stride=2), :]
    for copy in edges(0):
        copy.start()

    tile = ftile_ref[...]
    upper = ones_where(iota((128, 128), 0) <= iota((128, 128), 1)).astype(BF16)
    count = jnp.concatenate([upper, jnp.ones((128, 128), BF16)], axis=0)
    before = ones_where(iota((64, 64), 1) < iota((64, 64), 0)).astype(BF16)
    named = [ones_where(tile == t).astype(BF16) for t in range(TILES)]
    earlier = dot(before, jnp.concatenate(named, axis=1)).astype(BF16)
    ranks = dot(
        jnp.concatenate(
            [jnp.concatenate([named[t], earlier[:, 128 * t:128 * t + 128]], axis=1) for t in range(TILES)],
            axis=0),
        count)
    place = jnp.zeros((64, 128), F32)
    for t in range(TILES):
        place = jnp.where(tile == t, ranks[64 * t:64 * t + 64] + (512.0 * t - 1.0), place)
    place = place.astype(I32)
    cell = fcell_ref[...]
    elem = fel_ref[...]
    row = ((cell >> 7) & 63) * 2 + (cell >> 13)
    code = (row & 63) * 256 + (row >> 6) * 128 + (cell & 127)
    slot = iota((64, 128), 0) * 128 + iota((64, 128), 1)
    live = jnp.where(slot < fcount_ref[0], 128, 0)
    slot_tab[0] = (place >> 7).astype(F32)
    slot_tab[1] = (place & 127).astype(F32)
    slot_tab[2] = ((code >> 5) - 256).astype(F32)
    slot_tab[3] = ((code & 31) * 16 + (elem >> 7) - 256).astype(F32)
    slot_tab[4] = ((elem & 127) + live).astype(F32)

    row64 = iota((64, 128), 0).astype(F32)
    row128 = iota((128, 128), 0).astype(F32)

    def order_body(half, total):
        named = []
        inner = []
        for u in range(32):
            at = pl.ds(32 * half + u, 1)
            mine = row64 == slot_tab[0, at, :]
            named.append(jnp.concatenate(
                [jnp.where(mine, slot_tab[2 + v, at, :], 0.0).astype(BF16) for v in range(3)], axis=0))
            inner.append(ones_where(row128 == slot_tab[1, at, :]).astype(BF16))
        return total + dot_nt(jnp.concatenate(named, axis=1), jnp.concatenate(inner, axis=1))

    grouped = lax.fori_loop(0, 2, order_body, jnp.zeros((192, 128), F32)).astype(I32)
    middle = grouped[64:128] + 256
    code = ((grouped[0:64] + 256) * 32 + (middle >> 4)).astype(F32)
    high = ((middle & 15) + ((grouped[128:192] >> 7) << 4)).astype(F32)
    low = (grouped[128:192] & 127).astype(F32)
    for c in range(64):
        at = slice(128 * c, 128 * c + 128)
        inner = slice(128 * (c % 4), 128 * (c % 4) + 128)
        cells_out[c // 4, :, inner] = code[c:c + 1]
        elem_hi[:, at] = high[c:c + 1]
        elem_lo[:, at] = low[c:c + 1]
    start_all(cells_out, cells_in, cell_send, cell_recv)

    for k in range(4):
        hot[:, ELEMS * k:ELEMS * k + ELEMS] = units(256, nel_ref[k:k + 1, :] & 255)

    for k in range(4):
        at = slice(2048 * k, 2048 * k + 2048)
        elem_hot[:, at] = units(128, elem_lo[:, at].astype(I32))

    volume = stiff_ref[...] - exact_dot(lift, tmap)
    put_scores(scores_of(tr), 0)
    scale = STEP * jac_ref[...]
    own_state = s1[...]
    direct = jnp.sum(column(odir) * own_state, axis=0, keepdims=True)
    within = jnp.sum(column(exact_dot(odir, volume)) * own_state, axis=0, keepdims=True)

    for copy in pair(gout, grim, 6):
        copy.wait_recv()
    for side, got in enumerate(rims(grim)):
        put_scores(got, 8 + 4 * side)
    for k in range(4):
        at = slice(64 * k, 64 * k + 64)
        gh, gl = split(jnp.concatenate([gtab[0, at, :], gtab[1, at, :]], axis=1))
        got = dot(jnp.concatenate([gh, gl], axis=0), hot[:, ELEMS * k:ELEMS * k + ELEMS])
        mine = iota((64, ELEMS), 0) == nfa_ref[k:k + 1, :] * 16 + (nel_ref[k:k + 1, :] >> 8)
        within = within + jnp.sum(jnp.where(mine, got[0:64] + got[64:128], 0.0), axis=0, keepdims=True)
    score = direct + scale * within

    opening = 0.2 * (jnp.maximum(score, 0.0) + jnp.log1p(jnp.exp(-jnp.abs(score))))
    oh, ol = split(jnp.concatenate([opening[:, 128 * i:128 * i + 128] for i in range(16)], axis=0))
    got = dot(jnp.concatenate([oh, ol], axis=0), elem_hot[...])
    sixteen = (iota((16, 1), 0) + 16).astype(F32)
    picked = jnp.sum(
        jnp.where(sixteen == elem_hi[...], got[0:16] + got[16:32], 0.0), axis=0, keepdims=True)
    for t in range(TILES):
        open_out[t] = picked[:, 512 * t:512 * t + 512]
    start_all(open_out, open_in, open_send, open_recv)

    arrive_near(cells_out, cells_in, cell_send, cell_recv)
    arrive_far(cells_out, cells_in, cell_send, cell_recv)

    for t in range(TILES):
        at = slice(512 * t, 512 * t + 512)
        where = cells_in[t].astype(I32)
        cell_hot[:, at] = units(256, where & 255)
        cell_unit[:, at] = units(64, where >> 8)
        cell_row[:, at] = where >> 8

    row_i = iota((Q, 256), 0)
    col_i = iota((Q, 256), 1)
    own_block = ones_where(row_i == col_i).astype(BF16)
    blk = lax.div(col_i, QB)
    inner = lax.rem(col_i, QB)
    face_block = ones_where(
        (blk >= 1) & (blk <= 4) & (inner < Q) & (row_i == 9 * (blk - 1) + lax.rem(inner, 9))).astype(BF16)
    mh, ml = split(padded(volume, QB))
    lh, ll = split(padded(lift, QB))
    ww[0:QB, :] = (dot(mh, own_block) + dot(lh, face_block)).astype(BF16)
    ww[QB:2 * QB, :] = (dot(ml, own_block) + dot(ll, face_block)).astype(BF16)
    xh[5 * QB:256, :] = jnp.zeros((16, ELEMS), BF16)
    xl[5 * QB:256, :] = jnp.zeros((16, ELEMS), BF16)
    for copy in pair(out1, rim1, 0):
        copy.wait_recv()
    put_table(list(rims(rim1)), 8 * Q)
    gather_faces(0)

    def field_of(tiles):
        amounts = []
        for t in tiles:
            got = open_in[t]
            high = got.astype(BF16).astype(F32)
            unit = cell_unit[:, lanes(t, 512)]
            amounts.append(jnp.concatenate(
                [unit * jnp.concatenate([jnp.broadcast_to(part, (16, 512)).astype(BF16)] * 4, axis=0)
                 for part in (high, got - high)], axis=0))
        return dot_nt(
            jnp.concatenate(amounts, axis=1),
            jnp.concatenate([cell_hot[:, lanes(t, 512)] for t in tiles], axis=1))

    arrive_near(open_out, open_in, open_send, open_recv)
    field = field_of(near_tiles)
    arrive_far(open_out, open_in, open_send, open_recv)
    field = field + field_of(far_tiles)
    field = field[0:64] + field[64:128]
    aper = base_ref[...] + jnp.concatenate([field[:, 0:128], field[:, 128:256]], axis=0)
    aper_ref[...] = aper
    c = aper * aper * aper / 12.0
    cond[...] = c
    edge_out[2] = cond[pl.ds(0, 64, stride=2), :]
    edge_out[3] = cond[pl.ds(1, 64, stride=2), :]
    for copy in edges(1):
        copy.start()

    for k in range(1, 4):
        gather_faces(k)
    s1[...] = s1[...] + scale * change()

    p = press_ref[...]
    odd = (iota((128, 128), 0) & 1) == 1
    lane = iota((128, 128), 1)
    block = iota((128, 128), 0) >> 1
    for copy in edges(0) + edges(1):
        copy.wait_recv()
    for i in range(2):
        edge_wide[i, pl.ds(0, 64, stride=2), :] = edge_in[2 * i]
        edge_wide[i, pl.ds(1, 64, stride=2), :] = edge_in[2 * i + 1]

    def sides(x, wide):
        after = pltpu.roll(x, 127, 1)
        after = jnp.where(lane == 127, pltpu.roll(after, 126, 0), after)
        ahead = pltpu.roll(x, 1, 1)
        ahead = jnp.where(lane == 0, pltpu.roll(ahead, 2, 0), ahead)
        up = jnp.where(odd, pltpu.roll(x, 1, 0), wide)
        down = jnp.where(odd, wide, pltpu.roll(x, 127, 0))
        inside = (
            (lane < 127) | (block < 63),
            (lane > 0) | (block > 0),
            odd | (plane > 0),
            jnp.logical_not(odd) | (plane < TILES - 1),
        )
        return [jnp.where(m, v, 0.0) for m, v in zip(inside, (after, ahead, up, down))]

    inflow = jnp.zeros((128, 128), F32)
    for other_p, other_c in zip(sides(p, edge_wide[0]), sides(c, edge_wide[1])):
        inflow = inflow + 2.0 * c * other_c / (c + other_c) * (other_p - p)
    new_p = p + RATE * (inflow + inj_ref[...])
    new_press_ref[...] = new_p

    ph, prest = split(jnp.concatenate([new_p[0:64], new_p[64:128]], axis=1))
    pressures = jnp.concatenate([ph, prest], axis=0)
    for b in range(4):
        at = slice(2048 * b, 2048 * b + 2048)
        got = dot(pressures, cell_hot[:, at])
        mine = iota((64, 2048), 0) == cell_row[:, at]
        picked = jnp.sum(jnp.where(mine, got[0:64] + got[64:128], 0.0), axis=0, keepdims=True)
        for t in range(4):
            press_out[4 * b + t] = picked[:, 512 * t:512 * t + 512]
    start_all(press_out, press_in, pr_send, pr_recv)

    put_state(s1[...])
    put_table([traces()], 0)
    fill_outgoing(out2)
    for copy in pair(out2, rim2, 2):
        copy.start()
    for k in range(4):
        gather_own(k)

    push = column(tdir_ref[...])
    tau = exact_dot(tmap, push[0:Q])
    of_facet = jnp.where(lax.div(iota((Q, 128), 0), 9) == lax.rem(iota((Q, 128), 1), 4), tau, 0.0)
    spread = jnp.where(
        lax.div(iota((Q, 128), 0), 9) == lax.div(iota((Q, 128), 1), 4), exact_dot(same, of_facet), 0.0)
    load_map = jnp.where(
        iota((Q, 128), 1) == 16, exact_dot(volume, push[0:Q]), exact_dot(lift, spread))
    uh, ul = split(padded(load_map, QB))
    uu[0:QB, :] = uh
    uu[QB:2 * QB, :] = ul

    def load_of(tiles):
        high, rest = split(jnp.concatenate(
            [jnp.where(sixteen == elem_hi[:, lanes(t, 512)], press_in[t], 0.0) for t in tiles], axis=1))
        return dot_nt(
            jnp.concatenate([high, rest], axis=0),
            jnp.concatenate([elem_hot[:, lanes(t, 512)] for t in tiles], axis=1))

    arrive_near(press_out, press_in, pr_send, pr_recv)
    load = load_of(near_tiles)
    arrive_far(press_out, press_in, pr_send, pr_recv)
    load = load + load_of(far_tiles)
    load = load[0:16] + load[16:32]
    for i in range(16):
        lane_row[:, 128 * i:128 * i + 128] = load[i:i + 1]
    w = scale * lane_row[...]
    own_w = jnp.concatenate([w[:, 256 * l:256 * l + 256] for l in range(8)], axis=0)
    wh, wl = split(own_w)
    got = dot(jnp.concatenate([wh, wl], axis=0), send_hot[...])
    got = got[0:8] + got[8:16]
    for side in range(2):
        mine = iota((8, HALO), 0) == (send_ref[side:side + 1, :] >> 8)
        wout[side] = jnp.sum(
            jnp.where(mine, got[:, HALO * side:HALO * side + HALO], 0.0), axis=0, keepdims=True)
    for copy in pair(wout, wrim, 4):
        copy.start()
    for copy in pair(out2, rim2, 2):
        copy.wait_recv()
    put_table(list(rims(rim2)), 8 * Q)
    for k in range(4):
        gather_rims(k)
    change2 = change()
    for copy in pair(wout, wrim, 4):
        copy.wait_recv()
    low, high_rim = rims(wrim)
    far_w = jnp.concatenate([x[:, 256 * l:256 * l + 256] for x in (low, high_rim) for l in range(4)], axis=0)
    wh, wl = split(jnp.concatenate([own_w, far_w], axis=0))
    got = dot(jnp.concatenate([wh, wl], axis=0), hot[...])
    got = got[0:16] + got[16:32]
    near = []
    for k in range(4):
        mine = iota((16, ELEMS), 0) == (nel_ref[k:k + 1, :] >> 8)
        near_w = jnp.sum(jnp.where(mine, got[:, ELEMS * k:ELEMS * k + ELEMS], 0.0), axis=0, keepdims=True)
        near.append(jnp.where(iota((4, ELEMS), 0) == nfa_ref[k:k + 1, :], near_w, 0.0))
    near.append(w)
    near.append(jnp.zeros((128 - 17, ELEMS), F32))
    nh, nl = split(jnp.concatenate(near, axis=0))
    first = dot(uu[...], nh)
    extra = first[0:QP] + first[QB:QB + QP] + dot(uu[0:QB, :], nl)[0:QP]
    result = s1[...] + push * w + scale * (change2 + extra)
    new_state_ref[...] = result[0:Q]

    for index, (outs, ins) in enumerate(((out1, rim1), (out2, rim2), (wout, wrim), (gout, grim))):
        for copy in pair(outs, ins, 2 * index):
            copy.wait_send()
    for copy in edges(0) + edges(1):
        copy.wait_send()
    sent_all(cells_out, cells_in, cell_send, cell_recv)
    sent_all(open_out, open_in, open_send, open_recv)
    sent_all(press_out, press_in, pr_send, pr_recv)


def hand_over(*refs):
    copies = [pltpu.make_async_copy(refs[i], refs[3 + i], refs[6].at[i]) for i in range(3)]
    for copy in copies:
        copy.start()
    for copy in copies:
        copy.wait()


def interleaved(x):
    return x.reshape(2, 64, 128).transpose(1, 0, 2).reshape(128, 128)


def straight(x):
    return x.reshape(64, 2, 128).transpose(1, 0, 2).reshape(1, 2, 8192)


def shards(
    rock_state, jacobian, stiffness, trace_map, lift_map, neighbor_elem, neighbor_face, send_elem,
    opening_dir, traction_dir, face_elem, face_tile, face_cell, face_count, pressure, base_aperture, injection,
):
    vmem = pl.BlockSpec(memory_space=pltpu.VMEM)
    hbm = pl.BlockSpec(memory_space=pltpu.HBM)
    smem = pl.BlockSpec(memory_space=pltpu.SMEM)
    scratch = [
        pltpu.VMEM((QP, ELEMS), F32),
        pltpu.VMEM((16 * Q, 512), BF16),
        pltpu.VMEM((256, SLOTS), BF16),
        pltpu.VMEM((256, 2 * HALO), BF16),
        pltpu.VMEM((256, ELEMS), BF16),
        pltpu.VMEM((256, ELEMS), BF16),
        pltpu.VMEM((2 * QB, 256), BF16),
        pltpu.VMEM((2 * QB, QB), BF16),
        pltpu.VMEM((2 * QB, 128), BF16),
        pltpu.VMEM((32, QB), BF16),
        pltpu.VMEM((2, 256, 128), F32),
        pltpu.VMEM((2, QP, HALO), F32),
        pltpu.VMEM((2, QP, HALO), F32),
        pltpu.VMEM((2, QP, HALO), F32),
        pltpu.VMEM((2, QP, HALO), F32),
        pltpu.VMEM((2, 1, HALO), F32),
        pltpu.VMEM((2, 1, HALO), F32),
        pltpu.VMEM((2, 16, HALO), F32),
        pltpu.VMEM((2, 16, HALO), F32),
        pltpu.VMEM((128, SLOTS), BF16),
        pltpu.VMEM((1, SLOTS), F32),
        pltpu.VMEM((1, SLOTS), F32),
        pltpu.VMEM((TILES, 1, 512), F32),
        pltpu.VMEM((TILES, 1, 512), F32),
        pltpu.VMEM((TILES, 1, 512), F32),
        pltpu.VMEM((TILES, 1, 512), F32),
        pltpu.VMEM((TILES, 1, 512), F32),
        pltpu.VMEM((TILES, 1, 512), F32),
        pltpu.VMEM((5, 64, 128), F32),
        pltpu.VMEM((256, SLOTS), BF16),
        pltpu.VMEM((64, SLOTS), BF16),
        pltpu.VMEM((1, SLOTS), I32),
        pltpu.VMEM((128, 128), F32),
        pltpu.VMEM((4, 64, 128), F32),
        pltpu.VMEM((4, 64, 128), F32),
        pltpu.VMEM((2, 128, 128), F32),
        pltpu.VMEM((4, 2 * Q, ELEMS), F32),
        pltpu.VMEM((1, ELEMS), F32),
        pltpu.VMEM((Q, ELEMS), F32),
        pltpu.VMEM((1, ELEMS), F32),
        pltpu.VMEM((Q, Q), F32),
        pltpu.VMEM((Q, Q), F32),
        pltpu.VMEM((Q, Q), F32),
        pltpu.VMEM((4, ELEMS), I32),
        pltpu.VMEM((4, ELEMS), I32),
        pltpu.VMEM((2, HALO), I32),
        pltpu.VMEM((1, Q), F32),
        pltpu.VMEM((1, Q), F32),
        pltpu.VMEM((64, 128), I32),
        pltpu.VMEM((64, 128), I32),
        pltpu.VMEM((64, 128), I32),
        pltpu.VMEM((128, 128), F32),
        pltpu.VMEM((128, 128), F32),
        pltpu.VMEM((128, 128), F32),
    ] + [pltpu.SemaphoreType.DMA((n,)) for n in (16, 8, 8, 15, 15, 15, 15, 15, 15, 4, 4)]
    new_state, new_pressure, aperture = pl.pallas_call(
        kernel,
        out_shape=(
            pltpu.VMEM((Q, ELEMS), F32),
            pltpu.VMEM((128, 128), F32),
            pltpu.VMEM((128, 128), F32),
        ),
        in_specs=[hbm] * 13 + [smem] + [hbm] * 3,
        out_specs=(vmem,) * 3,
        scratch_shapes=scratch,
        compiler_params=pltpu.CompilerParams(
            collective_id=0, has_side_effects=True, vmem_limit_bytes=56 * 2**20),
    )(
        rock_state, jacobian.reshape(1, ELEMS), stiffness, trace_map, lift_map, neighbor_elem, neighbor_face,
        send_elem, opening_dir.reshape(1, Q), traction_dir.reshape(1, Q), face_elem.reshape(64, 128),
        face_tile.reshape(64, 128), face_cell.reshape(64, 128), face_count, interleaved(pressure),
        interleaved(base_aperture), interleaved(injection),
    )
    results = (new_state, new_pressure, aperture)
    new_state, new_pressure, aperture = pl.pallas_call(
        hand_over,
        out_shape=tuple(jax.ShapeDtypeStruct(x.shape, F32) for x in results),
        in_specs=[vmem] * 3,
        out_specs=(hbm,) * 3,
        scratch_shapes=[pltpu.SemaphoreType.DMA((3,))],
        compiler_params=pltpu.CompilerParams(vmem_limit_bytes=2**20),
    )(*results)
    return new_state, straight(new_pressure), straight(aperture)


def solution(mesh):
    elems = P(None, ("rock", "plane"))
    flat = P(("rock", "plane"))
    grid = P("rock", "plane", None)
    return jax.shard_map(
        shards,
        mesh=mesh,
        in_specs=(elems, flat, P(), P(), P(), elems, elems, elems, P(), P(), flat, flat, flat, flat, grid, grid, grid),
        out_specs=(elems, grid, grid),
        check_vma=False,
    )
```

```python
import jax
import jax.numpy as jnp
from jax import lax
from jax.experimental import pallas as pl
from jax.experimental.pallas import tpu as pltpu
from jax.sharding import PartitionSpec as P

STEP = 0.25
RATE = 0.35
F32 = jnp.float32
BF16 = jnp.bfloat16
I32 = jnp.int32
MESH = pl.DeviceIdType.MESH
Q = 36
QP = 40
QB = 48
ELEMS = 2048
HALO = 1024
SLOTS = 8192
TILES = 16
PARTS = 128
FAR = [(a, b) for a in (1, 2, 3) for b in (1, 2, 3)]
NEAR = [(0, 1), (0, 2), (0, 3), (1, 0), (2, 0), (3, 0)]
STEPS = FAR + NEAR


def dot(a, b):
    return jnp.dot(a, b, preferred_element_type=F32)


def dot_nt(a, b):
    return lax.dot_general(a, b, (((1,), (1,)), ((), ())), preferred_element_type=F32)


def exact_dot(a, b):
    return jnp.dot(a, b, preferred_element_type=F32, precision=lax.Precision.HIGHEST)


def split(x):
    high = x.astype(BF16)
    return high, (x - high.astype(F32)).astype(BF16)


def iota(shape, dim):
    return lax.broadcasted_iota(I32, shape, dim)


def ones_where(mask):
    return jnp.where(mask, 1.0, 0.0).astype(F32)


def units(count, row):
    return ones_where(iota((count, row.shape[1]), 0) == row).astype(BF16)


def lanes(chunk, width=128):
    return pl.ds(pl.multiple_of(chunk * width, width), width)


def padded(x, rows):
    return jnp.concatenate([x, jnp.zeros((rows - x.shape[0],) + x.shape[1:], x.dtype)], axis=0)


def column(row):
    wide = jnp.broadcast_to(row, (QP, Q))
    eye = iota((QP, Q), 0) == iota((QP, Q), 1)
    return jnp.sum(jnp.where(eye, wide, 0.0), axis=1, keepdims=True)


def kernel(
    state_hbm, jac_hbm, stiff_hbm, tmap_hbm, lift_hbm, nel_hbm, nfa_hbm, send_hbm, odir_hbm, tdir_hbm,
    fel_hbm, ftile_hbm, fcell_hbm, fcount_ref, press_hbm, base_hbm, inj_hbm,
    new_state_ref, new_press_ref, aper_ref,
    s1, table, hot, send_hot, xh, xl, ww, tw, uu, gw, gtab, out1, out2, rim1, rim2, wout, wrim, gout, grim,
    elem_hot, elem_hi, elem_lo, cells_out, cells_in, open_out, open_in, press_out, press_in,
    slot_tab, cell_hot, cell_unit, cell_row, cond, edge_out, edge_in, edge_wide, own2, lane_row,
    state_ref, jac_ref, stiff_ref, tmap_ref, lift_ref, nel_ref, nfa_ref, send_ref, odir_ref, tdir_ref,
    fel_ref, ftile_ref, fcell_ref, press_ref, base_ref, inj_ref, in_sem,
    halo_send, halo_recv, cell_send, cell_recv, open_send, open_recv, pr_send, pr_recv, edge_send, edge_recv,
):
    loads = [
        pltpu.make_async_copy(source, target, in_sem.at[i])
        for i, (source, target) in enumerate((
            (state_hbm, state_ref), (tmap_hbm, tmap_ref), (send_hbm, send_ref), (lift_hbm, lift_ref),
            (odir_hbm, odir_ref), (ftile_hbm, ftile_ref), (fcell_hbm, fcell_ref), (fel_hbm, fel_ref), (press_hbm, press_ref),
            (nel_hbm, nel_ref), (nfa_hbm, nfa_ref), (stiff_hbm, stiff_ref),
            (jac_hbm, jac_ref), (tdir_hbm, tdir_ref), (base_hbm, base_ref), (inj_hbm, inj_ref)))
    ]
    loads[0].start()
    rock = lax.axis_index("rock")
    plane = lax.axis_index("plane")
    here = rock * TILES + plane
    nxt = lax.rem(here + 1, PARTS)
    prv = lax.rem(here + PARTS - 1, PARTS)
    next_part = (lax.div(nxt, TILES), lax.rem(nxt, TILES))
    prev_part = (lax.div(prv, TILES), lax.rem(prv, TILES))
    next_tile = (rock, lax.rem(plane + 1, TILES))
    prev_tile = (rock, lax.rem(plane + TILES - 1, TILES))

    def tile_at(a, b):
        return lax.rem(lax.div(plane, 4) + a, 4) * 4 + lax.rem(lax.rem(plane, 4) + b, 4)

    targets = [tile_at(a, b) for a, b in STEPS]
    sources = [tile_at(4 - a, 4 - b) for a, b in STEPS]
    far_tiles = sources[:len(FAR)]
    near_tiles = [plane] + sources[len(FAR):]

    barrier = pltpu.get_barrier_semaphore()

    def greet(target):
        pl.semaphore_signal(barrier, inc=1, device_id=target, device_id_type=MESH)

    pl.when(here < PARTS - 1)(lambda: greet(next_part))
    pl.when(here > 0)(lambda: greet(prev_part))

    for target in targets:
        greet((rock, target))
    for load in loads[1:]:
        load.start()

    def pair(outs, ins, index):
        return [
            pltpu.make_async_remote_copy(
                outs.at[0], ins.at[1], halo_send.at[index], halo_recv.at[index],
                device_id=prev_part, device_id_type=MESH),
            pltpu.make_async_remote_copy(
                outs.at[1], ins.at[0], halo_send.at[index + 1], halo_recv.at[index + 1],
                device_id=next_part, device_id_type=MESH),
        ]

    def start_pair(*what):
        down, up = pair(*what)
        pl.when(here > 0)(down.start)
        pl.when(here < PARTS - 1)(up.start)

    def arrive_pair(*what):
        down, up = pair(*what)
        pl.when(here < PARTS - 1)(down.wait_recv)
        pl.when(here > 0)(up.wait_recv)

    def sent_pair(*what):
        down, up = pair(*what)
        pl.when(here > 0)(down.wait_send)
        pl.when(here < PARTS - 1)(up.wait_send)

    @pl.when(here == 0)
    def _():
        for rim in (grim, rim1, rim2, wrim):
            rim[0] = jnp.zeros(rim.shape[1:], F32)

    @pl.when(here == PARTS - 1)
    def _():
        for rim in (grim, rim1, rim2, wrim):
            rim[1] = jnp.zeros(rim.shape[1:], F32)

    def edges(index):
        return [
            pltpu.make_async_remote_copy(
                edge_out.at[2 * index], edge_in.at[2 * index + 1], edge_send.at[2 * index],
                edge_recv.at[2 * index], device_id=prev_tile, device_id_type=MESH),
            pltpu.make_async_remote_copy(
                edge_out.at[2 * index + 1], edge_in.at[2 * index], edge_send.at[2 * index + 1],
                edge_recv.at[2 * index + 1], device_id=next_tile, device_id_type=MESH),
        ]

    def swap(outs, ins, sends, recvs, o):
        return pltpu.make_async_remote_copy(
            outs.at[targets[o]], ins.at[plane], sends.at[o], recvs.at[o],
            device_id=(rock, targets[o]), device_id_type=MESH)

    def start_all(*what):
        for o in range(len(STEPS)):
            swap(*what, o).start()
        outs, ins = what[:2]
        ins[plane] = outs[plane]

    def arrive_far(*what):
        for o in range(len(FAR)):
            swap(*what, o).wait_recv()

    def arrive_near(*what):
        for o in range(len(FAR), len(STEPS)):
            swap(*what, o).wait_recv()

    def sent_all(*what):
        for o in range(len(STEPS)):
            swap(*what, o).wait_send()

    for load in loads[:5]:
        load.wait()
    tmap = tmap_ref[...]
    lift = lift_ref[...]
    widen = ones_where(iota((Q, QB), 0) == iota((Q, QB), 1)).astype(BF16)
    th, tl = split(padded(tmap, QB))
    tw[0:QB, :] = dot(th, widen).astype(BF16)
    tw[QB:2 * QB, :] = dot(tl, widen).astype(BF16)

    same = ones_where(lax.rem(iota((Q, Q), 0), 9) == lax.rem(iota((Q, Q), 1), 9))
    odir = odir_ref[...]
    of_face = jnp.where(lax.div(iota((16, Q), 0), 4) == lax.div(iota((16, Q), 1), 9), exact_dot(odir, lift), 0.0)
    of_face = exact_dot(of_face, same)
    gh, gl = split(jnp.where(lax.rem(iota((16, Q), 0), 4) == lax.div(iota((16, Q), 1), 9), of_face, 0.0))
    gw[0:16, :] = dot(gh, widen).astype(BF16)
    gw[16:32, :] = dot(gl, widen).astype(BF16)

    def scores_of(x):
        high, rest = split(padded(x, QB))
        got = dot(gw[...], high)
        return got[0:16] + got[16:32] + dot(gw[0:16, :], rest)

    def put_scores(got, start):
        for l in range(got.shape[1] // 256):
            for half in range(2):
                at = 256 * l + 128 * half
                gtab[half, pl.ds(start + l, 16, stride=16), :] = got[:, at:at + 128]

    def put_state(x):
        high, rest = split(padded(x, QB))
        xh[0:QB, :] = high
        xl[0:QB, :] = rest

    def traces():
        first = dot(tw[...], xh[0:QB, :])
        return first[0:QP] + first[QB:QB + QP] + dot(tw[0:QB, :], xl[0:QB, :])[0:QP]

    def put_table(parts, start):
        rows = jnp.concatenate(
            [x[0:Q, 256 * l:256 * l + 256] for x in parts for l in range(x.shape[1] // 256)], axis=0)
        high, rest = split(rows)
        table[start:start + rows.shape[0], 0:256] = high
        table[start:start + rows.shape[0], 256:512] = rest

    def pick(got, rows, which, first, count):
        for l in range(count // 2):
            part = rows[2 * Q * l:2 * Q * l + 2 * Q]
            got = part if got is None else jnp.where((which >> 1) == first // 2 + l, part, got)
        return got

    def one_of(got, which):
        return jnp.where((which & 1) == 1, got[Q:2 * Q], got[0:Q])

    def fill_outgoing(out):
        for side in range(2):
            a = send_hot[:, HALO * side:HALO * side + HALO]
            which = send_ref[side:side + 1, :] >> 8
            rows = dot(table[0:8 * Q, :], jnp.concatenate([a, a], axis=0))
            out[side] = padded(one_of(pick(None, rows, which, 0, 8), which), QP)

    face_of_row = lax.div(iota((Q, 1), 0), 9)

    def columns(k, rows):
        a = hot[:, ELEMS * k:ELEMS * k + ELEMS]
        return dot(rows, jnp.concatenate([a, a], axis=0))

    def put_faces(k, got):
        got = jnp.where(face_of_row == nfa_ref[k:k + 1, :], got, 0.0)
        high, rest = split(padded(got, QB))
        xh[QB * (k + 1):QB * (k + 2), :] = high
        xl[QB * (k + 1):QB * (k + 2), :] = rest

    def gather_faces(k):
        which = nel_ref[k:k + 1, :] >> 8
        put_faces(k, one_of(pick(None, columns(k, table[...]), which, 0, 16), which))

    def gather_own(k):
        own2[k] = pick(None, columns(k, table[0:8 * Q, :]), nel_ref[k:k + 1, :] >> 8, 0, 8)

    def gather_rims(k):
        which = nel_ref[k:k + 1, :] >> 8
        put_faces(k, one_of(pick(own2[k], columns(k, table[8 * Q:, :]), which, 8, 8), which))

    def change():
        first = dot(ww[...], xh[...])
        return first[0:QP] + first[QB:QB + QP] + dot(ww[0:QB, :], xl[...])[0:QP]

    s1[0:Q, :] = state_ref[...]
    s1[Q:QP, :] = jnp.zeros((QP - Q, ELEMS), F32)
    put_state(s1[...])
    tr = traces()
    put_table([tr], 0)

    for side in range(2):
        send_hot[:, HALO * side:HALO * side + HALO] = units(256, send_ref[side:side + 1, :] & 255)
    fill_outgoing(out1)
    for side in range(2):
        gout[side] = scores_of(out1[side])
    both = lax.div(here + PARTS - 2, PARTS - 1) + lax.div(2 * PARTS - 3 - here, PARTS - 1)
    pl.semaphore_wait(barrier, TILES - 1 + both)
    start_pair(gout, grim, 6)
    start_pair(out1, rim1, 0)
    for load in loads[5:]:
        load.wait()
    edge_out[0] = press_ref[pl.ds(0, 64, stride=2), :]
    edge_out[1] = press_ref[pl.ds(1, 64, stride=2), :]
    for copy in edges(0):
        copy.start()

    tile = ftile_ref[...]
    upper = ones_where(iota((128, 128), 0) <= iota((128, 128), 1)).astype(BF16)
    count = jnp.concatenate([upper, jnp.ones((128, 128), BF16)], axis=0)
    before = ones_where(iota((64, 64), 1) < iota((64, 64), 0)).astype(BF16)
    named = [ones_where(tile == t).astype(BF16) for t in range(TILES)]
    earlier = dot(before, jnp.concatenate(named, axis=1)).astype(BF16)
    ranks = dot(
        jnp.concatenate(
            [jnp.concatenate([named[t], earlier[:, 128 * t:128 * t + 128]], axis=1) for t in range(TILES)],
            axis=0),
        count)
    place = jnp.zeros((64, 128), F32)
    for t in range(TILES):
        place = jnp.where(tile == t, ranks[64 * t:64 * t + 64] + (512.0 * t - 1.0), place)
    place = place.astype(I32)
    cell = fcell_ref[...]
    elem = fel_ref[...]
    row = ((cell >> 7) & 63) * 2 + (cell >> 13)
    code = (row & 63) * 256 + (row >> 6) * 128 + (cell & 127)
    slot = iota((64, 128), 0) * 128 + iota((64, 128), 1)
    live = jnp.where(slot < fcount_ref[0], 128, 0)
    slot_tab[0] = (place >> 7).astype(F32)
    slot_tab[1] = (place & 127).astype(F32)
    slot_tab[2] = ((code >> 5) - 256).astype(F32)
    slot_tab[3] = ((code & 31) * 16 + (elem >> 7) - 256).astype(F32)
    slot_tab[4] = ((elem & 127) + live).astype(F32)

    row64 = iota((64, 128), 0).astype(F32)
    row128 = iota((128, 128), 0).astype(F32)

    def order_body(half, total):
        named = []
        inner = []
        for u in range(32):
            at = pl.ds(32 * half + u, 1)
            mine = row64 == slot_tab[0, at, :]
            named.append(jnp.concatenate(
                [jnp.where(mine, slot_tab[2 + v, at, :], 0.0).astype(BF16) for v in range(3)], axis=0))
            inner.append(ones_where(row128 == slot_tab[1, at, :]).astype(BF16))
        return total + dot_nt(jnp.concatenate(named, axis=1), jnp.concatenate(inner, axis=1))

    grouped = lax.fori_loop(0, 2, order_body, jnp.zeros((192, 128), F32)).astype(I32)
    middle = grouped[64:128] + 256
    code = ((grouped[0:64] + 256) * 32 + (middle >> 4)).astype(F32)
    high = ((middle & 15) + ((grouped[128:192] >> 7) << 4)).astype(F32)
    low = (grouped[128:192] & 127).astype(F32)
    for c in range(64):
        at = slice(128 * c, 128 * c + 128)
        inner = slice(128 * (c % 4), 128 * (c % 4) + 128)
        cells_out[c // 4, :, inner] = code[c:c + 1]
        elem_hi[:, at] = high[c:c + 1]
        elem_lo[:, at] = low[c:c + 1]
    start_all(cells_out, cells_in, cell_send, cell_recv)

    for k in range(4):
        hot[:, ELEMS * k:ELEMS * k + ELEMS] = units(256, nel_ref[k:k + 1, :] & 255)

    for k in range(4):
        at = slice(2048 * k, 2048 * k + 2048)
        elem_hot[:, at] = units(128, elem_lo[:, at].astype(I32))

    volume = stiff_ref[...] - exact_dot(lift, tmap)
    put_scores(scores_of(tr), 0)
    scale = STEP * jac_ref[...]
    own_state = s1[...]
    direct = jnp.sum(column(odir) * own_state, axis=0, keepdims=True)
    within = jnp.sum(column(exact_dot(odir, volume)) * own_state, axis=0, keepdims=True)

    arrive_pair(gout, grim, 6)
    for side in range(2):
        put_scores(grim[side], 8 + 4 * side)
    for k in range(4):
        at = slice(64 * k, 64 * k + 64)
        gh, gl = split(jnp.concatenate([gtab[0, at, :], gtab[1, at, :]], axis=1))
        got = dot(jnp.concatenate([gh, gl], axis=0), hot[:, ELEMS * k:ELEMS * k + ELEMS])
        mine = iota((64, ELEMS), 0) == nfa_ref[k:k + 1, :] * 16 + (nel_ref[k:k + 1, :] >> 8)
        within = within + jnp.sum(jnp.where(mine, got[0:64] + got[64:128], 0.0), axis=0, keepdims=True)
    score = direct + scale * within

    opening = 0.2 * (jnp.maximum(score, 0.0) + jnp.log1p(jnp.exp(-jnp.abs(score))))
    oh, ol = split(jnp.concatenate([opening[:, 128 * i:128 * i + 128] for i in range(16)], axis=0))
    got = dot(jnp.concatenate([oh, ol], axis=0), elem_hot[...])
    sixteen = (iota((16, 1), 0) + 16).astype(F32)
    picked = jnp.sum(
        jnp.where(sixteen == elem_hi[...], got[0:16] + got[16:32], 0.0), axis=0, keepdims=True)
    for t in range(TILES):
        open_out[t] = picked[:, 512 * t:512 * t + 512]
    start_all(open_out, open_in, open_send, open_recv)

    arrive_near(cells_out, cells_in, cell_send, cell_recv)
    arrive_far(cells_out, cells_in, cell_send, cell_recv)

    for t in range(TILES):
        at = slice(512 * t, 512 * t + 512)
        where = cells_in[t].astype(I32)
        cell_hot[:, at] = units(256, where & 255)
        cell_unit[:, at] = units(64, where >> 8)
        cell_row[:, at] = where >> 8

    row_i = iota((Q, 256), 0)
    col_i = iota((Q, 256), 1)
    own_block = ones_where(row_i == col_i).astype(BF16)
    blk = lax.div(col_i, QB)
    inner = lax.rem(col_i, QB)
    face_block = ones_where(
        (blk >= 1) & (blk <= 4) & (inner < Q) & (row_i == 9 * (blk - 1) + lax.rem(inner, 9))).astype(BF16)
    mh, ml = split(padded(volume, QB))
    lh, ll = split(padded(lift, QB))
    ww[0:QB, :] = (dot(mh, own_block) + dot(lh, face_block)).astype(BF16)
    ww[QB:2 * QB, :] = (dot(ml, own_block) + dot(ll, face_block)).astype(BF16)
    xh[5 * QB:256, :] = jnp.zeros((16, ELEMS), BF16)
    xl[5 * QB:256, :] = jnp.zeros((16, ELEMS), BF16)
    arrive_pair(out1, rim1, 0)
    put_table([rim1[0], rim1[1]], 8 * Q)
    gather_faces(0)

    def field_of(tiles):
        amounts = []
        for t in tiles:
            got = open_in[t]
            high = got.astype(BF16).astype(F32)
            unit = cell_unit[:, lanes(t, 512)]
            amounts.append(jnp.concatenate(
                [unit * jnp.concatenate([jnp.broadcast_to(part, (16, 512)).astype(BF16)] * 4, axis=0)
                 for part in (high, got - high)], axis=0))
        return dot_nt(
            jnp.concatenate(amounts, axis=1),
            jnp.concatenate([cell_hot[:, lanes(t, 512)] for t in tiles], axis=1))

    arrive_near(open_out, open_in, open_send, open_recv)
    field = field_of(near_tiles)
    arrive_far(open_out, open_in, open_send, open_recv)
    field = field + field_of(far_tiles)
    field = field[0:64] + field[64:128]
    aper = base_ref[...] + jnp.concatenate([field[:, 0:128], field[:, 128:256]], axis=0)
    aper_ref[...] = aper
    c = aper * aper * aper / 12.0
    cond[...] = c
    edge_out[2] = cond[pl.ds(0, 64, stride=2), :]
    edge_out[3] = cond[pl.ds(1, 64, stride=2), :]
    for copy in edges(1):
        copy.start()

    for k in range(1, 4):
        gather_faces(k)
    s1[...] = s1[...] + scale * change()

    p = press_ref[...]
    odd = (iota((128, 128), 0) & 1) == 1
    lane = iota((128, 128), 1)
    block = iota((128, 128), 0) >> 1
    for copy in edges(0) + edges(1):
        copy.wait_recv()
    for i in range(2):
        edge_wide[i, pl.ds(0, 64, stride=2), :] = edge_in[2 * i]
        edge_wide[i, pl.ds(1, 64, stride=2), :] = edge_in[2 * i + 1]

    def sides(x, wide):
        after = pltpu.roll(x, 127, 1)
        after = jnp.where(lane == 127, pltpu.roll(after, 126, 0), after)
        ahead = pltpu.roll(x, 1, 1)
        ahead = jnp.where(lane == 0, pltpu.roll(ahead, 2, 0), ahead)
        up = jnp.where(odd, pltpu.roll(x, 1, 0), wide)
        down = jnp.where(odd, wide, pltpu.roll(x, 127, 0))
        inside = (
            (lane < 127) | (block < 63),
            (lane > 0) | (block > 0),
            odd | (plane > 0),
            jnp.logical_not(odd) | (plane < TILES - 1),
        )
        return [jnp.where(m, v, 0.0) for m, v in zip(inside, (after, ahead, up, down))]

    inflow = jnp.zeros((128, 128), F32)
    for other_p, other_c in zip(sides(p, edge_wide[0]), sides(c, edge_wide[1])):
        inflow = inflow + 2.0 * c * other_c / (c + other_c) * (other_p - p)
    new_p = p + RATE * (inflow + inj_ref[...])
    new_press_ref[...] = new_p

    ph, prest = split(jnp.concatenate([new_p[0:64], new_p[64:128]], axis=1))
    pressures = jnp.concatenate([ph, prest], axis=0)
    for b in range(4):
        at = slice(2048 * b, 2048 * b + 2048)
        got = dot(pressures, cell_hot[:, at])
        mine = iota((64, 2048), 0) == cell_row[:, at]
        picked = jnp.sum(jnp.where(mine, got[0:64] + got[64:128], 0.0), axis=0, keepdims=True)
        for t in range(4):
            press_out[4 * b + t] = picked[:, 512 * t:512 * t + 512]
    start_all(press_out, press_in, pr_send, pr_recv)

    put_state(s1[...])
    put_table([traces()], 0)
    fill_outgoing(out2)
    start_pair(out2, rim2, 2)
    for k in range(4):
        gather_own(k)


    def load_of(tiles):
        high, rest = split(jnp.concatenate(
            [jnp.where(sixteen == elem_hi[:, lanes(t, 512)], press_in[t], 0.0) for t in tiles], axis=1))
        return dot_nt(
            jnp.concatenate([high, rest], axis=0),
            jnp.concatenate([elem_hot[:, lanes(t, 512)] for t in tiles], axis=1))

    arrive_near(press_out, press_in, pr_send, pr_recv)
    load = load_of(near_tiles)
    arrive_far(press_out, press_in, pr_send, pr_recv)
    load = load + load_of(far_tiles)
    load = load[0:16] + load[16:32]
    for i in range(16):
        lane_row[:, 128 * i:128 * i + 128] = load[i:i + 1]
    w = scale * lane_row[...]
    own_w = jnp.concatenate([w[:, 256 * l:256 * l + 256] for l in range(8)], axis=0)
    wh, wl = split(own_w)
    got = dot(jnp.concatenate([wh, wl], axis=0), send_hot[...])
    got = got[0:8] + got[8:16]
    for side in range(2):
        mine = iota((8, HALO), 0) == (send_ref[side:side + 1, :] >> 8)
        wout[side] = jnp.sum(
            jnp.where(mine, got[:, HALO * side:HALO * side + HALO], 0.0), axis=0, keepdims=True)
    start_pair(wout, wrim, 4)
    push = column(tdir_ref[...])
    tau = exact_dot(tmap, push[0:Q])
    of_facet = jnp.where(lax.div(iota((Q, 128), 0), 9) == lax.rem(iota((Q, 128), 1), 4), tau, 0.0)
    spread = jnp.where(
        lax.div(iota((Q, 128), 0), 9) == lax.div(iota((Q, 128), 1), 4), exact_dot(same, of_facet), 0.0)
    load_map = jnp.where(
        iota((Q, 128), 1) == 16, exact_dot(volume, push[0:Q]), exact_dot(lift, spread))
    uh, ul = split(padded(load_map, QB))
    uu[0:QB, :] = uh
    uu[QB:2 * QB, :] = ul
    arrive_pair(out2, rim2, 2)
    put_table([rim2[0], rim2[1]], 8 * Q)
    for k in range(4):
        gather_rims(k)
    result = s1[...] + push * w + scale * change()
    arrive_pair(wout, wrim, 4)
    far_w = jnp.concatenate([wrim[side, :, 256 * l:256 * l + 256] for side in range(2) for l in range(4)], axis=0)
    wh, wl = split(jnp.concatenate([own_w, far_w], axis=0))
    got = dot(jnp.concatenate([wh, wl], axis=0), hot[...])
    got = got[0:16] + got[16:32]
    near = []
    for k in range(4):
        mine = iota((16, ELEMS), 0) == (nel_ref[k:k + 1, :] >> 8)
        near_w = jnp.sum(jnp.where(mine, got[:, ELEMS * k:ELEMS * k + ELEMS], 0.0), axis=0, keepdims=True)
        near.append(jnp.where(iota((4, ELEMS), 0) == nfa_ref[k:k + 1, :], near_w, 0.0))
    near.append(w)
    near.append(jnp.zeros((128 - 17, ELEMS), F32))
    nh, nl = split(jnp.concatenate(near, axis=0))
    first = dot(uu[...], nh)
    extra = first[0:QP] + first[QB:QB + QP] + dot(uu[0:QB, :], nl)[0:QP]
    new_state_ref[...] = (result + scale * extra)[0:Q]

    for index, (outs, ins) in enumerate(((out1, rim1), (out2, rim2), (wout, wrim), (gout, grim))):
        sent_pair(outs, ins, 2 * index)
    for copy in edges(0) + edges(1):
        copy.wait_send()
    sent_all(cells_out, cells_in, cell_send, cell_recv)
    sent_all(open_out, open_in, open_send, open_recv)
    sent_all(press_out, press_in, pr_send, pr_recv)


def hand_over(*refs):
    copies = [pltpu.make_async_copy(refs[i], refs[3 + i], refs[6].at[i]) for i in range(3)]
    for copy in copies:
        copy.start()
    for copy in copies:
        copy.wait()


def interleaved(x):
    return x.reshape(2, 64, 128).transpose(1, 0, 2).reshape(128, 128)


def straight(x):
    return x.reshape(64, 2, 128).transpose(1, 0, 2).reshape(1, 2, 8192)


def shards(
    rock_state, jacobian, stiffness, trace_map, lift_map, neighbor_elem, neighbor_face, send_elem,
    opening_dir, traction_dir, face_elem, face_tile, face_cell, face_count, pressure, base_aperture, injection,
):
    vmem = pl.BlockSpec(memory_space=pltpu.VMEM)
    hbm = pl.BlockSpec(memory_space=pltpu.HBM)
    smem = pl.BlockSpec(memory_space=pltpu.SMEM)
    scratch = [
        pltpu.VMEM((QP, ELEMS), F32),
        pltpu.VMEM((16 * Q, 512), BF16),
        pltpu.VMEM((256, SLOTS), BF16),
        pltpu.VMEM((256, 2 * HALO), BF16),
        pltpu.VMEM((256, ELEMS), BF16),
        pltpu.VMEM((256, ELEMS), BF16),
        pltpu.VMEM((2 * QB, 256), BF16),
        pltpu.VMEM((2 * QB, QB), BF16),
        pltpu.VMEM((2 * QB, 128), BF16),
        pltpu.VMEM((32, QB), BF16),
        pltpu.VMEM((2, 256, 128), F32),
        pltpu.VMEM((2, QP, HALO), F32),
        pltpu.VMEM((2, QP, HALO), F32),
        pltpu.VMEM((2, QP, HALO), F32),
        pltpu.VMEM((2, QP, HALO), F32),
        pltpu.VMEM((2, 1, HALO), F32),
        pltpu.VMEM((2, 1, HALO), F32),
        pltpu.VMEM((2, 16, HALO), F32),
        pltpu.VMEM((2, 16, HALO), F32),
        pltpu.VMEM((128, SLOTS), BF16),
        pltpu.VMEM((1, SLOTS), F32),
        pltpu.VMEM((1, SLOTS), F32),
        pltpu.VMEM((TILES, 1, 512), F32),
        pltpu.VMEM((TILES, 1, 512), F32),
        pltpu.VMEM((TILES, 1, 512), F32),
        pltpu.VMEM((TILES, 1, 512), F32),
        pltpu.VMEM((TILES, 1, 512), F32),
        pltpu.VMEM((TILES, 1, 512), F32),
        pltpu.VMEM((5, 64, 128), F32),
        pltpu.VMEM((256, SLOTS), BF16),
        pltpu.VMEM((64, SLOTS), BF16),
        pltpu.VMEM((1, SLOTS), I32),
        pltpu.VMEM((128, 128), F32),
        pltpu.VMEM((4, 64, 128), F32),
        pltpu.VMEM((4, 64, 128), F32),
        pltpu.VMEM((2, 128, 128), F32),
        pltpu.VMEM((4, 2 * Q, ELEMS), F32),
        pltpu.VMEM((1, ELEMS), F32),
        pltpu.VMEM((Q, ELEMS), F32),
        pltpu.VMEM((1, ELEMS), F32),
        pltpu.VMEM((Q, Q), F32),
        pltpu.VMEM((Q, Q), F32),
        pltpu.VMEM((Q, Q), F32),
        pltpu.VMEM((4, ELEMS), I32),
        pltpu.VMEM((4, ELEMS), I32),
        pltpu.VMEM((2, HALO), I32),
        pltpu.VMEM((1, Q), F32),
        pltpu.VMEM((1, Q), F32),
        pltpu.VMEM((64, 128), I32),
        pltpu.VMEM((64, 128), I32),
        pltpu.VMEM((64, 128), I32),
        pltpu.VMEM((128, 128), F32),
        pltpu.VMEM((128, 128), F32),
        pltpu.VMEM((128, 128), F32),
    ] + [pltpu.SemaphoreType.DMA((n,)) for n in (16, 8, 8, 15, 15, 15, 15, 15, 15, 4, 4)]
    new_state, new_pressure, aperture = pl.pallas_call(
        kernel,
        out_shape=(
            pltpu.VMEM((Q, ELEMS), F32),
            pltpu.VMEM((128, 128), F32),
            pltpu.VMEM((128, 128), F32),
        ),
        in_specs=[hbm] * 13 + [smem] + [hbm] * 3,
        out_specs=(vmem,) * 3,
        scratch_shapes=scratch,
        compiler_params=pltpu.CompilerParams(
            collective_id=0, has_side_effects=True, vmem_limit_bytes=56 * 2**20),
    )(
        rock_state, jacobian.reshape(1, ELEMS), stiffness, trace_map, lift_map, neighbor_elem, neighbor_face,
        send_elem, opening_dir.reshape(1, Q), traction_dir.reshape(1, Q), face_elem.reshape(64, 128),
        face_tile.reshape(64, 128), face_cell.reshape(64, 128), face_count, interleaved(pressure),
        interleaved(base_aperture), interleaved(injection),
    )
    results = (new_state, new_pressure, aperture)
    new_state, new_pressure, aperture = pl.pallas_call(
        hand_over,
        out_shape=tuple(jax.ShapeDtypeStruct(x.shape, F32) for x in results),
        in_specs=[vmem] * 3,
        out_specs=(hbm,) * 3,
        scratch_shapes=[pltpu.SemaphoreType.DMA((3,))],
        compiler_params=pltpu.CompilerParams(vmem_limit_bytes=2**20),
    )(*results)
    return new_state, straight(new_pressure), straight(aperture)


def solution(mesh):
    elems = P(None, ("rock", "plane"))
    flat = P(("rock", "plane"))
    grid = P("rock", "plane", None)
    return jax.shard_map(
        shards,
        mesh=mesh,
        in_specs=(elems, flat, P(), P(), P(), elems, elems, elems, P(), P(), flat, flat, flat, flat, grid, grid, grid),
        out_specs=(elems, grid, grid),
        check_vma=False,
    )
```

```python
import jax
import jax.numpy as jnp
from jax import lax
from jax.experimental import pallas as pl
from jax.experimental.pallas import tpu as pltpu
from jax.sharding import PartitionSpec as P

STEP = 0.25
RATE = 0.35
F32 = jnp.float32
BF16 = jnp.bfloat16
I32 = jnp.int32
MESH = pl.DeviceIdType.MESH
Q = 36
QP = 40
QB = 48
ELEMS = 2048
HALO = 1024
SLOTS = 8192
TILES = 16
PARTS = 128
FAR = [(a, b) for a in (1, 2, 3) for b in (1, 2, 3)]
NEAR = [(0, 1), (0, 2), (0, 3), (1, 0), (2, 0), (3, 0)]
STEPS = FAR + NEAR


def dot(a, b):
    return jnp.dot(a, b, preferred_element_type=F32)


def dot_nt(a, b):
    return lax.dot_general(a, b, (((1,), (1,)), ((), ())), preferred_element_type=F32)


def exact_dot(a, b):
    return jnp.dot(a, b, preferred_element_type=F32, precision=lax.Precision.HIGHEST)


def split(x):
    high = x.astype(BF16)
    return high, (x - high.astype(F32)).astype(BF16)


def iota(shape, dim):
    return lax.broadcasted_iota(I32, shape, dim)


def ones_where(mask):
    return jnp.where(mask, 1.0, 0.0).astype(F32)


def units(count, row):
    shape = (count, row.shape[1])
    row = jnp.broadcast_to(row.astype(F32), (16, shape[1])).astype(BF16)
    same = iota(shape, 0).astype(F32).astype(BF16) == jnp.concatenate([row] * (count // 16), axis=0)
    return jnp.where(same, jnp.ones((), BF16), jnp.zeros((), BF16))


def lanes(chunk, width=128):
    return pl.ds(pl.multiple_of(chunk * width, width), width)


def padded(x, rows):
    return jnp.concatenate([x, jnp.zeros((rows - x.shape[0],) + x.shape[1:], x.dtype)], axis=0)


def column(row):
    wide = jnp.broadcast_to(row, (QP, Q))
    eye = iota((QP, Q), 0) == iota((QP, Q), 1)
    return jnp.sum(jnp.where(eye, wide, 0.0), axis=1, keepdims=True)


def kernel(
    state_hbm, jac_hbm, stiff_hbm, tmap_hbm, lift_hbm, nel_hbm, nfa_hbm, send_hbm, odir_hbm, tdir_hbm,
    fel_hbm, ftile_hbm, fcell_hbm, fcount_ref, press_hbm, base_hbm, inj_hbm,
    new_state_ref, new_press_ref, aper_ref,
    s1, table, hot, send_hot, xh, xl, ww, tw, uu, gw, gtab, out1, out2, rim1, rim2, wout, wrim, gout, grim,
    elem_hot, elem_hi, elem_lo, cells_out, cells_in, open_out, open_in, press_out, press_in,
    slot_tab, cell_hot, cell_unit, cell_row, cond, edge_out, edge_in, edge_wide, own2, lane_row,
    state_ref, jac_ref, stiff_ref, tmap_ref, lift_ref, nel_ref, nfa_ref, send_ref, odir_ref, tdir_ref,
    fel_ref, ftile_ref, fcell_ref, press_ref, base_ref, inj_ref, in_sem,
    halo_send, halo_recv, cell_send, cell_recv, open_send, open_recv, pr_send, pr_recv, edge_send, edge_recv,
):
    loads = [
        pltpu.make_async_copy(source, target, in_sem.at[i])
        for i, (source, target) in enumerate((
            (state_hbm, state_ref), (tmap_hbm, tmap_ref), (send_hbm, send_ref), (lift_hbm, lift_ref),
            (odir_hbm, odir_ref), (ftile_hbm, ftile_ref), (fcell_hbm, fcell_ref), (fel_hbm, fel_ref), (press_hbm, press_ref),
            (nel_hbm, nel_ref), (nfa_hbm, nfa_ref), (stiff_hbm, stiff_ref),
            (jac_hbm, jac_ref), (tdir_hbm, tdir_ref), (base_hbm, base_ref), (inj_hbm, inj_ref)))
    ]
    loads[0].start()
    rock = lax.axis_index("rock")
    plane = lax.axis_index("plane")
    here = rock * TILES + plane
    nxt = lax.rem(here + 1, PARTS)
    prv = lax.rem(here + PARTS - 1, PARTS)
    next_part = (lax.div(nxt, TILES), lax.rem(nxt, TILES))
    prev_part = (lax.div(prv, TILES), lax.rem(prv, TILES))
    next_tile = (rock, lax.rem(plane + 1, TILES))
    prev_tile = (rock, lax.rem(plane + TILES - 1, TILES))

    def tile_at(a, b):
        return lax.rem(lax.div(plane, 4) + a, 4) * 4 + lax.rem(lax.rem(plane, 4) + b, 4)

    targets = [tile_at(a, b) for a, b in STEPS]
    sources = [tile_at(4 - a, 4 - b) for a, b in STEPS]
    far_tiles = sources[:len(FAR)]
    near_tiles = [plane] + sources[len(FAR):]

    barrier = pltpu.get_barrier_semaphore()

    def greet(target):
        pl.semaphore_signal(barrier, inc=1, device_id=target, device_id_type=MESH)

    pl.when(here < PARTS - 1)(lambda: greet(next_part))
    pl.when(here > 0)(lambda: greet(prev_part))

    for target in targets:
        greet((rock, target))
    for load in loads[1:]:
        load.start()

    def pair(outs, ins, index):
        return [
            pltpu.make_async_remote_copy(
                outs.at[0], ins.at[1], halo_send.at[index], halo_recv.at[index],
                device_id=prev_part, device_id_type=MESH),
            pltpu.make_async_remote_copy(
                outs.at[1], ins.at[0], halo_send.at[index + 1], halo_recv.at[index + 1],
                device_id=next_part, device_id_type=MESH),
        ]

    def start_pair(*what):
        down, up = pair(*what)
        pl.when(here > 0)(down.start)
        pl.when(here < PARTS - 1)(up.start)

    def arrive_pair(*what):
        down, up = pair(*what)
        pl.when(here < PARTS - 1)(down.wait_recv)
        pl.when(here > 0)(up.wait_recv)

    def sent_pair(*what):
        down, up = pair(*what)
        pl.when(here > 0)(down.wait_send)
        pl.when(here < PARTS - 1)(up.wait_send)

    @pl.when(here == 0)
    def _():
        for rim in (grim, rim1, rim2, wrim):
            rim[0] = jnp.zeros(rim.shape[1:], F32)

    @pl.when(here == PARTS - 1)
    def _():
        for rim in (grim, rim1, rim2, wrim):
            rim[1] = jnp.zeros(rim.shape[1:], F32)

    def edges(index):
        return [
            pltpu.make_async_remote_copy(
                edge_out.at[2 * index], edge_in.at[2 * index + 1], edge_send.at[2 * index],
                edge_recv.at[2 * index], device_id=prev_tile, device_id_type=MESH),
            pltpu.make_async_remote_copy(
                edge_out.at[2 * index + 1], edge_in.at[2 * index], edge_send.at[2 * index + 1],
                edge_recv.at[2 * index + 1], device_id=next_tile, device_id_type=MESH),
        ]

    def swap(outs, ins, sends, recvs, o):
        return pltpu.make_async_remote_copy(
            outs.at[targets[o]], ins.at[plane], sends.at[o], recvs.at[o],
            device_id=(rock, targets[o]), device_id_type=MESH)

    def start_all(*what):
        for o in range(len(STEPS)):
            swap(*what, o).start()
        outs, ins = what[:2]
        ins[plane] = outs[plane]

    def arrive_far(*what):
        for o in range(len(FAR)):
            swap(*what, o).wait_recv()

    def arrive_near(*what):
        for o in range(len(FAR), len(STEPS)):
            swap(*what, o).wait_recv()

    def sent_all(*what):
        for o in range(len(STEPS)):
            swap(*what, o).wait_send()

    for load in loads[:5]:
        load.wait()
    tmap = tmap_ref[...]
    lift = lift_ref[...]
    widen = ones_where(iota((Q, QB), 0) == iota((Q, QB), 1)).astype(BF16)
    th, tl = split(padded(tmap, QB))
    tw[0:QB, :] = dot(th, widen).astype(BF16)
    tw[QB:2 * QB, :] = dot(tl, widen).astype(BF16)

    same = ones_where(lax.rem(iota((Q, Q), 0), 9) == lax.rem(iota((Q, Q), 1), 9))
    odir = odir_ref[...]
    of_face = jnp.where(lax.div(iota((16, Q), 0), 4) == lax.div(iota((16, Q), 1), 9), exact_dot(odir, lift), 0.0)
    of_face = exact_dot(of_face, same)
    gh, gl = split(jnp.where(lax.rem(iota((16, Q), 0), 4) == lax.div(iota((16, Q), 1), 9), of_face, 0.0))
    gw[0:16, :] = dot(gh, widen).astype(BF16)
    gw[16:32, :] = dot(gl, widen).astype(BF16)

    def scores_of(x):
        high, rest = split(padded(x, QB))
        got = dot(gw[...], high)
        return got[0:16] + got[16:32] + dot(gw[0:16, :], rest)

    def put_scores(got, start):
        for l in range(got.shape[1] // 256):
            for half in range(2):
                at = 256 * l + 128 * half
                gtab[half, pl.ds(start + l, 16, stride=16), :] = got[:, at:at + 128]

    def put_state(x):
        high, rest = split(padded(x, QB))
        xh[0:QB, :] = high
        xl[0:QB, :] = rest

    def traces():
        first = dot(tw[...], xh[0:QB, :])
        return first[0:QP] + first[QB:QB + QP] + dot(tw[0:QB, :], xl[0:QB, :])[0:QP]

    def put_table(parts, start):
        rows = jnp.concatenate(
            [x[0:Q, 256 * l:256 * l + 256] for x in parts for l in range(x.shape[1] // 256)], axis=0)
        high, rest = split(rows)
        table[start:start + rows.shape[0], 0:256] = high
        table[start:start + rows.shape[0], 256:512] = rest

    def pick(got, rows, which, first, count):
        for l in range(count // 2):
            part = rows[2 * Q * l:2 * Q * l + 2 * Q]
            got = part if got is None else jnp.where((which >> 1) == first // 2 + l, part, got)
        return got

    def one_of(got, which):
        return jnp.where((which & 1) == 1, got[Q:2 * Q], got[0:Q])

    def fill_outgoing(out):
        for side in range(2):
            a = send_hot[:, HALO * side:HALO * side + HALO]
            which = send_ref[side:side + 1, :] >> 8
            rows = dot(table[0:8 * Q, :], jnp.concatenate([a, a], axis=0))
            out[side] = padded(one_of(pick(None, rows, which, 0, 8), which), QP)

    face_of_row = lax.div(iota((Q, 1), 0), 9)

    def columns(k, rows):
        a = hot[:, ELEMS * k:ELEMS * k + ELEMS]
        return dot(rows, jnp.concatenate([a, a], axis=0))

    def put_faces(k, got):
        got = jnp.where(face_of_row == nfa_ref[k:k + 1, :], got, 0.0)
        high, rest = split(padded(got, QB))
        xh[QB * (k + 1):QB * (k + 2), :] = high
        xl[QB * (k + 1):QB * (k + 2), :] = rest

    def gather_faces(k):
        which = nel_ref[k:k + 1, :] >> 8
        put_faces(k, one_of(pick(None, columns(k, table[...]), which, 0, 16), which))

    def gather_own(k):
        own2[k] = pick(None, columns(k, table[0:8 * Q, :]), nel_ref[k:k + 1, :] >> 8, 0, 8)

    def gather_rims(k):
        which = nel_ref[k:k + 1, :] >> 8
        put_faces(k, one_of(pick(own2[k], columns(k, table[8 * Q:, :]), which, 8, 8), which))

    def change():
        first = dot(ww[...], xh[...])
        return first[0:QP] + first[QB:QB + QP] + dot(ww[0:QB, :], xl[...])[0:QP]

    s1[0:Q, :] = state_ref[...]
    s1[Q:QP, :] = jnp.zeros((QP - Q, ELEMS), F32)
    put_state(s1[...])
    tr = traces()
    put_table([tr], 0)

    for side in range(2):
        send_hot[:, HALO * side:HALO * side + HALO] = units(256, send_ref[side:side + 1, :] & 255)
    fill_outgoing(out1)
    for side in range(2):
        gout[side] = scores_of(out1[side])
    both = lax.div(here + PARTS - 2, PARTS - 1) + lax.div(2 * PARTS - 3 - here, PARTS - 1)
    pl.semaphore_wait(barrier, TILES - 1 + both)
    start_pair(gout, grim, 6)
    start_pair(out1, rim1, 0)
    for load in loads[5:]:
        load.wait()
    edge_out[0] = press_ref[pl.ds(0, 64, stride=2), :]
    edge_out[1] = press_ref[pl.ds(1, 64, stride=2), :]
    for copy in edges(0):
        copy.start()

    tile = ftile_ref[...]
    upper = ones_where(iota((128, 128), 0) <= iota((128, 128), 1)).astype(BF16)
    count = jnp.concatenate([upper, jnp.ones((128, 128), BF16)], axis=0)
    before = ones_where(iota((64, 64), 1) < iota((64, 64), 0)).astype(BF16)
    named = [ones_where(tile == t).astype(BF16) for t in range(TILES)]
    earlier = dot(before, jnp.concatenate(named, axis=1)).astype(BF16)
    ranks = dot(
        jnp.concatenate(
            [jnp.concatenate([named[t], earlier[:, 128 * t:128 * t + 128]], axis=1) for t in range(TILES)],
            axis=0),
        count)
    place = jnp.zeros((64, 128), F32)
    for t in range(TILES):
        place = jnp.where(tile == t, ranks[64 * t:64 * t + 64] + (512.0 * t - 1.0), place)
    place = place.astype(I32)
    cell = fcell_ref[...]
    elem = fel_ref[...]
    row = ((cell >> 7) & 63) * 2 + (cell >> 13)
    code = (row & 63) * 256 + (row >> 6) * 128 + (cell & 127)
    slot = iota((64, 128), 0) * 128 + iota((64, 128), 1)
    live = jnp.where(slot < fcount_ref[0], 128, 0)
    slot_tab[0] = (place >> 7).astype(F32)
    slot_tab[1] = (place & 127).astype(F32)
    slot_tab[2] = ((code >> 5) - 256).astype(F32)
    slot_tab[3] = ((code & 31) * 16 + (elem >> 7) - 256).astype(F32)
    slot_tab[4] = ((elem & 127) + live).astype(F32)

    row64 = iota((64, 128), 0).astype(F32)
    row128 = iota((128, 128), 0).astype(F32)

    def order_body(half, total):
        named = []
        inner = []
        for u in range(32):
            at = pl.ds(32 * half + u, 1)
            mine = row64 == slot_tab[0, at, :]
            named.append(jnp.concatenate(
                [jnp.where(mine, slot_tab[2 + v, at, :], 0.0).astype(BF16) for v in range(3)], axis=0))
            inner.append(ones_where(row128 == slot_tab[1, at, :]).astype(BF16))
        return total + dot_nt(jnp.concatenate(named, axis=1), jnp.concatenate(inner, axis=1))

    grouped = lax.fori_loop(0, 2, order_body, jnp.zeros((192, 128), F32)).astype(I32)
    middle = grouped[64:128] + 256
    code = ((grouped[0:64] + 256) * 32 + (middle >> 4)).astype(F32)
    high = ((middle & 15) + ((grouped[128:192] >> 7) << 4)).astype(F32)
    low = (grouped[128:192] & 127).astype(F32)
    for c in range(64):
        at = slice(128 * c, 128 * c + 128)
        inner = slice(128 * (c % 4), 128 * (c % 4) + 128)
        cells_out[c // 4, :, inner] = code[c:c + 1]
        elem_hi[:, at] = high[c:c + 1]
        elem_lo[:, at] = low[c:c + 1]
    start_all(cells_out, cells_in, cell_send, cell_recv)

    for k in range(4):
        hot[:, ELEMS * k:ELEMS * k + ELEMS] = units(256, nel_ref[k:k + 1, :] & 255)

    for k in range(4):
        at = slice(2048 * k, 2048 * k + 2048)
        elem_hot[:, at] = units(128, elem_lo[:, at].astype(I32))

    volume = stiff_ref[...] - exact_dot(lift, tmap)
    put_scores(scores_of(tr), 0)
    scale = STEP * jac_ref[...]
    own_state = s1[...]
    direct = jnp.sum(column(odir) * own_state, axis=0, keepdims=True)
    within = jnp.sum(column(exact_dot(odir, volume)) * own_state, axis=0, keepdims=True)

    arrive_pair(gout, grim, 6)
    for side in range(2):
        put_scores(grim[side], 8 + 4 * side)
    for k in range(4):
        at = slice(64 * k, 64 * k + 64)
        gh, gl = split(jnp.concatenate([gtab[0, at, :], gtab[1, at, :]], axis=1))
        got = dot(jnp.concatenate([gh, gl], axis=0), hot[:, ELEMS * k:ELEMS * k + ELEMS])
        mine = iota((64, ELEMS), 0) == nfa_ref[k:k + 1, :] * 16 + (nel_ref[k:k + 1, :] >> 8)
        within = within + jnp.sum(jnp.where(mine, got[0:64] + got[64:128], 0.0), axis=0, keepdims=True)
    score = direct + scale * within

    opening = 0.2 * (jnp.maximum(score, 0.0) + jnp.log1p(jnp.exp(-jnp.abs(score))))
    oh, ol = split(jnp.concatenate([opening[:, 128 * i:128 * i + 128] for i in range(16)], axis=0))
    got = dot(jnp.concatenate([oh, ol], axis=0), elem_hot[...])
    sixteen = (iota((16, 1), 0) + 16).astype(F32)
    picked = jnp.sum(
        jnp.where(sixteen == elem_hi[...], got[0:16] + got[16:32], 0.0), axis=0, keepdims=True)
    for t in range(TILES):
        open_out[t] = picked[:, 512 * t:512 * t + 512]
    start_all(open_out, open_in, open_send, open_recv)

    arrive_near(cells_out, cells_in, cell_send, cell_recv)
    arrive_far(cells_out, cells_in, cell_send, cell_recv)

    for t in range(TILES):
        at = slice(512 * t, 512 * t + 512)
        where = cells_in[t].astype(I32)
        cell_hot[:, at] = units(256, where & 255)
        cell_unit[:, at] = units(64, where >> 8)
        cell_row[:, at] = where >> 8

    row_i = iota((Q, 256), 0)
    col_i = iota((Q, 256), 1)
    own_block = ones_where(row_i == col_i).astype(BF16)
    blk = lax.div(col_i, QB)
    inner = lax.rem(col_i, QB)
    face_block = ones_where(
        (blk >= 1) & (blk <= 4) & (inner < Q) & (row_i == 9 * (blk - 1) + lax.rem(inner, 9))).astype(BF16)
    mh, ml = split(padded(volume, QB))
    lh, ll = split(padded(lift, QB))
    ww[0:QB, :] = (dot(mh, own_block) + dot(lh, face_block)).astype(BF16)
    ww[QB:2 * QB, :] = (dot(ml, own_block) + dot(ll, face_block)).astype(BF16)
    xh[5 * QB:256, :] = jnp.zeros((16, ELEMS), BF16)
    xl[5 * QB:256, :] = jnp.zeros((16, ELEMS), BF16)
    arrive_pair(out1, rim1, 0)
    put_table([rim1[0], rim1[1]], 8 * Q)
    gather_faces(0)

    def field_of(tiles):
        amounts = []
        for t in tiles:
            got = open_in[t]
            high = got.astype(BF16).astype(F32)
            unit = cell_unit[:, lanes(t, 512)]
            amounts.append(jnp.concatenate(
                [unit * jnp.concatenate([jnp.broadcast_to(part, (16, 512)).astype(BF16)] * 4, axis=0)
                 for part in (high, got - high)], axis=0))
        return dot_nt(
            jnp.concatenate(amounts, axis=1),
            jnp.concatenate([cell_hot[:, lanes(t, 512)] for t in tiles], axis=1))

    arrive_near(open_out, open_in, open_send, open_recv)
    field = field_of(near_tiles)
    arrive_far(open_out, open_in, open_send, open_recv)
    field = field + field_of(far_tiles)
    field = field[0:64] + field[64:128]
    aper = base_ref[...] + jnp.concatenate([field[:, 0:128], field[:, 128:256]], axis=0)
    aper_ref[...] = aper
    c = aper * aper * aper / 12.0
    cond[...] = c
    edge_out[2] = cond[pl.ds(0, 64, stride=2), :]
    edge_out[3] = cond[pl.ds(1, 64, stride=2), :]
    for copy in edges(1):
        copy.start()

    for k in range(1, 4):
        gather_faces(k)
    s1[...] = s1[...] + scale * change()

    p = press_ref[...]
    odd = (iota((128, 128), 0) & 1) == 1
    lane = iota((128, 128), 1)
    block = iota((128, 128), 0) >> 1
    for copy in edges(0) + edges(1):
        copy.wait_recv()
    for i in range(2):
        edge_wide[i, pl.ds(0, 64, stride=2), :] = edge_in[2 * i]
        edge_wide[i, pl.ds(1, 64, stride=2), :] = edge_in[2 * i + 1]

    def sides(x, wide):
        after = pltpu.roll(x, 127, 1)
        after = jnp.where(lane == 127, pltpu.roll(after, 126, 0), after)
        ahead = pltpu.roll(x, 1, 1)
        ahead = jnp.where(lane == 0, pltpu.roll(ahead, 2, 0), ahead)
        up = jnp.where(odd, pltpu.roll(x, 1, 0), wide)
        down = jnp.where(odd, wide, pltpu.roll(x, 127, 0))
        inside = (
            (lane < 127) | (block < 63),
            (lane > 0) | (block > 0),
            odd | (plane > 0),
            jnp.logical_not(odd) | (plane < TILES - 1),
        )
        return [jnp.where(m, v, 0.0) for m, v in zip(inside, (after, ahead, up, down))]

    inflow = jnp.zeros((128, 128), F32)
    for other_p, other_c in zip(sides(p, edge_wide[0]), sides(c, edge_wide[1])):
        inflow = inflow + 2.0 * c * other_c / (c + other_c) * (other_p - p)
    new_p = p + RATE * (inflow + inj_ref[...])
    new_press_ref[...] = new_p

    ph, prest = split(jnp.concatenate([new_p[0:64], new_p[64:128]], axis=1))
    pressures = jnp.concatenate([ph, prest], axis=0)
    for b in range(4):
        at = slice(2048 * b, 2048 * b + 2048)
        got = dot(pressures, cell_hot[:, at])
        mine = iota((64, 2048), 0) == cell_row[:, at]
        picked = jnp.sum(jnp.where(mine, got[0:64] + got[64:128], 0.0), axis=0, keepdims=True)
        for t in range(4):
            press_out[4 * b + t] = picked[:, 512 * t:512 * t + 512]
    start_all(press_out, press_in, pr_send, pr_recv)

    put_state(s1[...])
    put_table([traces()], 0)
    fill_outgoing(out2)
    start_pair(out2, rim2, 2)
    for k in range(4):
        gather_own(k)


    def load_of(tiles):
        high, rest = split(jnp.concatenate(
            [jnp.where(sixteen == elem_hi[:, lanes(t, 512)], press_in[t], 0.0) for t in tiles], axis=1))
        return dot_nt(
            jnp.concatenate([high, rest], axis=0),
            jnp.concatenate([elem_hot[:, lanes(t, 512)] for t in tiles], axis=1))

    arrive_near(press_out, press_in, pr_send, pr_recv)
    load = load_of(near_tiles)
    arrive_far(press_out, press_in, pr_send, pr_recv)
    load = load + load_of(far_tiles)
    load = load[0:16] + load[16:32]
    for i in range(16):
        lane_row[:, 128 * i:128 * i + 128] = load[i:i + 1]
    w = scale * lane_row[...]
    own_w = jnp.concatenate([w[:, 256 * l:256 * l + 256] for l in range(8)], axis=0)
    wh, wl = split(own_w)
    got = dot(jnp.concatenate([wh, wl], axis=0), send_hot[...])
    got = got[0:8] + got[8:16]
    for side in range(2):
        mine = iota((8, HALO), 0) == (send_ref[side:side + 1, :] >> 8)
        wout[side] = jnp.sum(
            jnp.where(mine, got[:, HALO * side:HALO * side + HALO], 0.0), axis=0, keepdims=True)
    start_pair(wout, wrim, 4)
    push = column(tdir_ref[...])
    tau = exact_dot(tmap, push[0:Q])
    of_facet = jnp.where(lax.div(iota((Q, 128), 0), 9) == lax.rem(iota((Q, 128), 1), 4), tau, 0.0)
    spread = jnp.where(
        lax.div(iota((Q, 128), 0), 9) == lax.div(iota((Q, 128), 1), 4), exact_dot(same, of_facet), 0.0)
    load_map = jnp.where(
        iota((Q, 128), 1) == 16, exact_dot(volume, push[0:Q]), exact_dot(lift, spread))
    uh, ul = split(padded(load_map, QB))
    uu[0:QB, :] = uh
    uu[QB:2 * QB, :] = ul
    arrive_pair(out2, rim2, 2)
    put_table([rim2[0], rim2[1]], 8 * Q)
    for k in range(4):
        gather_rims(k)
    result = s1[...] + push * w + scale * change()
    arrive_pair(wout, wrim, 4)
    far_w = jnp.concatenate([wrim[side, :, 256 * l:256 * l + 256] for side in range(2) for l in range(4)], axis=0)
    wh, wl = split(jnp.concatenate([own_w, far_w], axis=0))
    got = dot(jnp.concatenate([wh, wl], axis=0), hot[...])
    got = got[0:16] + got[16:32]
    near = []
    for k in range(4):
        mine = iota((16, ELEMS), 0) == (nel_ref[k:k + 1, :] >> 8)
        near_w = jnp.sum(jnp.where(mine, got[:, ELEMS * k:ELEMS * k + ELEMS], 0.0), axis=0, keepdims=True)
        near.append(jnp.where(iota((4, ELEMS), 0) == nfa_ref[k:k + 1, :], near_w, 0.0))
    near.append(w)
    near.append(jnp.zeros((128 - 17, ELEMS), F32))
    nh, nl = split(jnp.concatenate(near, axis=0))
    first = dot(uu[...], nh)
    extra = first[0:QP] + first[QB:QB + QP] + dot(uu[0:QB, :], nl)[0:QP]
    new_state_ref[...] = (result + scale * extra)[0:Q]

    for index, (outs, ins) in enumerate(((out1, rim1), (out2, rim2), (wout, wrim), (gout, grim))):
        sent_pair(outs, ins, 2 * index)
    for copy in edges(0) + edges(1):
        copy.wait_send()
    sent_all(cells_out, cells_in, cell_send, cell_recv)
    sent_all(open_out, open_in, open_send, open_recv)
    sent_all(press_out, press_in, pr_send, pr_recv)


def hand_over(*refs):
    copies = [pltpu.make_async_copy(refs[i], refs[3 + i], refs[6].at[i]) for i in range(3)]
    for copy in copies:
        copy.start()
    for copy in copies:
        copy.wait()


def interleaved(x):
    return x.reshape(2, 64, 128).transpose(1, 0, 2).reshape(128, 128)


def straight(x):
    return x.reshape(64, 2, 128).transpose(1, 0, 2).reshape(1, 2, 8192)


def shards(
    rock_state, jacobian, stiffness, trace_map, lift_map, neighbor_elem, neighbor_face, send_elem,
    opening_dir, traction_dir, face_elem, face_tile, face_cell, face_count, pressure, base_aperture, injection,
):
    vmem = pl.BlockSpec(memory_space=pltpu.VMEM)
    hbm = pl.BlockSpec(memory_space=pltpu.HBM)
    smem = pl.BlockSpec(memory_space=pltpu.SMEM)
    scratch = [
        pltpu.VMEM((QP, ELEMS), F32),
        pltpu.VMEM((16 * Q, 512), BF16),
        pltpu.VMEM((256, SLOTS), BF16),
        pltpu.VMEM((256, 2 * HALO), BF16),
        pltpu.VMEM((256, ELEMS), BF16),
        pltpu.VMEM((256, ELEMS), BF16),
        pltpu.VMEM((2 * QB, 256), BF16),
        pltpu.VMEM((2 * QB, QB), BF16),
        pltpu.VMEM((2 * QB, 128), BF16),
        pltpu.VMEM((32, QB), BF16),
        pltpu.VMEM((2, 256, 128), F32),
        pltpu.VMEM((2, QP, HALO), F32),
        pltpu.VMEM((2, QP, HALO), F32),
        pltpu.VMEM((2, QP, HALO), F32),
        pltpu.VMEM((2, QP, HALO), F32),
        pltpu.VMEM((2, 1, HALO), F32),
        pltpu.VMEM((2, 1, HALO), F32),
        pltpu.VMEM((2, 16, HALO), F32),
        pltpu.VMEM((2, 16, HALO), F32),
        pltpu.VMEM((128, SLOTS), BF16),
        pltpu.VMEM((1, SLOTS), F32),
        pltpu.VMEM((1, SLOTS), F32),
        pltpu.VMEM((TILES, 1, 512), F32),
        pltpu.VMEM((TILES, 1, 512), F32),
        pltpu.VMEM((TILES, 1, 512), F32),
        pltpu.VMEM((TILES, 1, 512), F32),
        pltpu.VMEM((TILES, 1, 512), F32),
        pltpu.VMEM((TILES, 1, 512), F32),
        pltpu.VMEM((5, 64, 128), F32),
        pltpu.VMEM((256, SLOTS), BF16),
        pltpu.VMEM((64, SLOTS), BF16),
        pltpu.VMEM((1, SLOTS), I32),
        pltpu.VMEM((128, 128), F32),
        pltpu.VMEM((4, 64, 128), F32),
        pltpu.VMEM((4, 64, 128), F32),
        pltpu.VMEM((2, 128, 128), F32),
        pltpu.VMEM((4, 2 * Q, ELEMS), F32),
        pltpu.VMEM((1, ELEMS), F32),
        pltpu.VMEM((Q, ELEMS), F32),
        pltpu.VMEM((1, ELEMS), F32),
        pltpu.VMEM((Q, Q), F32),
        pltpu.VMEM((Q, Q), F32),
        pltpu.VMEM((Q, Q), F32),
        pltpu.VMEM((4, ELEMS), I32),
        pltpu.VMEM((4, ELEMS), I32),
        pltpu.VMEM((2, HALO), I32),
        pltpu.VMEM((1, Q), F32),
        pltpu.VMEM((1, Q), F32),
        pltpu.VMEM((64, 128), I32),
        pltpu.VMEM((64, 128), I32),
        pltpu.VMEM((64, 128), I32),
        pltpu.VMEM((128, 128), F32),
        pltpu.VMEM((128, 128), F32),
        pltpu.VMEM((128, 128), F32),
    ] + [pltpu.SemaphoreType.DMA((n,)) for n in (16, 8, 8, 15, 15, 15, 15, 15, 15, 4, 4)]
    new_state, new_pressure, aperture = pl.pallas_call(
        kernel,
        out_shape=(
            pltpu.VMEM((Q, ELEMS), F32),
            pltpu.VMEM((128, 128), F32),
            pltpu.VMEM((128, 128), F32),
        ),
        in_specs=[hbm] * 13 + [smem] + [hbm] * 3,
        out_specs=(vmem,) * 3,
        scratch_shapes=scratch,
        compiler_params=pltpu.CompilerParams(
            collective_id=0, has_side_effects=True, vmem_limit_bytes=56 * 2**20),
    )(
        rock_state, jacobian.reshape(1, ELEMS), stiffness, trace_map, lift_map, neighbor_elem, neighbor_face,
        send_elem, opening_dir.reshape(1, Q), traction_dir.reshape(1, Q), face_elem.reshape(64, 128),
        face_tile.reshape(64, 128), face_cell.reshape(64, 128), face_count, interleaved(pressure),
        interleaved(base_aperture), interleaved(injection),
    )
    results = (new_state, new_pressure, aperture)
    new_state, new_pressure, aperture = pl.pallas_call(
        hand_over,
        out_shape=tuple(jax.ShapeDtypeStruct(x.shape, F32) for x in results),
        in_specs=[vmem] * 3,
        out_specs=(hbm,) * 3,
        scratch_shapes=[pltpu.SemaphoreType.DMA((3,))],
        compiler_params=pltpu.CompilerParams(vmem_limit_bytes=2**20),
    )(*results)
    return new_state, straight(new_pressure), straight(aperture)


def solution(mesh):
    elems = P(None, ("rock", "plane"))
    flat = P(("rock", "plane"))
    grid = P("rock", "plane", None)
    return jax.shard_map(
        shards,
        mesh=mesh,
        in_specs=(elems, flat, P(), P(), P(), elems, elems, elems, P(), P(), flat, flat, flat, flat, grid, grid, grid),
        out_specs=(elems, grid, grid),
        check_vma=False,
    )
```
